512 devices in a mesh: group: 64 (over z, x), tensor: 8 (over y, core).
Axes of the slice: x: 4, y: 4, z: 16, core: 2. Of those that a mesh axis runs over, the one named last changes fastest.
Arguments:
- tokens: bfloat16 [32768, 2048], P('group', 'tensor')
- w_query: bfloat16 [2048, 2048], P('group', 'tensor'), may hold values from -0.125 to 0.125
- w_key: bfloat16 [2048, 2048], P('group', 'tensor'), may hold values from -0.125 to 0.125
- w_value: bfloat16 [2048, 2048], P('group', 'tensor'), may hold values from -0.125 to 0.125
- w_out: bfloat16 [2048, 2048], P('tensor', 'group'), may hold values from -0.125 to 0.125
- prefix_cache: bfloat16 [64, 2, 512, 2048], P('group', None, None, 'tensor')
- prefix_len: int32 [64], P('group'), may hold values from 0 to 512, as said below
- owners: int32 [4096, 1], P('group'), may hold values from 0 to 63; in each aligned block of 64 rows (0 to 63, 64 to 127, ...) at most 2 rows name the same one
Outputs:
- attn_out: bfloat16 [32768, 2048], P('group', 'tensor')
- decode_cache: bfloat16 [64, 128, 2, 16, 2048], P('group', None, None, None, 'tensor')
The draws below stay inside these ranges and needn't reach their ends.
Inputs may be any that keep to these rules, and one draw needn't show every extreme that they name: `owners`: every prompt sends at most 2 blocks to one owner, and exactly 2 to some owner. `prefix_len`: some prompt fills all 512 slots.
All inputs are finite; a program needn't handle non-finite values.
Results may differ from the reference program's by a relative error of at most 0.02.
The reference program's roundings to bfloat16 on the way count: a program that leaves them out, or rounds other values in their place, can miss the bound.
Values may be sent and summed in bfloat16 or wider, within the bound.
A program may use at most 64 MiB of HBM per device.

```python
import math
import jax
import jax.numpy as jnp
import numpy as np
from jax import lax

D = 2048
H = 16
HD = 128
NEW_TOK = 512
PRE = 512
BT = 16
NBLK = 64
CAP = 2
N_GROUP = 64


def draw_tokens(key, part):
    key = jax.random.fold_in(key, 11)
    return jax.random.normal(key, (N_GROUP * NEW_TOK, D), jnp.float32).astype(jnp.bfloat16)


def draw_prefix_cache(key, part):
    key = jax.random.fold_in(key, 23)
    return jax.random.normal(key, (N_GROUP, 2, PRE, H * HD), jnp.float32).astype(jnp.bfloat16)


def draw_prefix_len(key, part):
    key = jax.random.fold_in(key, 37)
    first, second = jax.random.split(key)
    lengths = jax.random.randint(first, (N_GROUP,), 0, PRE + 1)
    full_at = jax.random.randint(second, (), 0, N_GROUP)
    return lengths.at[full_at].set(PRE).astype(jnp.int32)


def levels(own_key, dims, pieces, least, high):
    def one(dim, shards_of):
        heights = jax.random.uniform(jax.random.fold_in(jax.random.fold_in(own_key, 6), dim), (shards_of,), jnp.float32, least / len(pieces), high / len(pieces))
        return jnp.repeat(jnp.exp(heights), dims[dim] // shards_of).reshape((-1,) + (1,) * (len(dims) - dim - 1))

    loudness = one(*pieces[0])
    for cut in pieces[1:]:
        loudness = loudness * one(*cut)
    return loudness


def assign_block(stream_key, own, number, rows, count, top, bound, skew):
    order = jax.random.permutation(stream_key, count)
    packed, ordinary = portions_of(count, rows * top, bound, skew, True), portions_of(count, rows * top, bound, skew, False)
    places = jnp.arange(count)

    def named(sizes, offset_by):
        used = int((sizes > 0).sum())
        fixed = max(1, used // 4)
        passed = fixed + (places - fixed + offset_by * (used - fixed)) % max(1, count - fixed)
        return jnp.zeros((count,), jnp.int32).at[order[jnp.where(places < fixed, places, passed)]].set(jnp.asarray(sizes, jnp.int32))

    sizes = jnp.where(number % 4 == 0, named(packed, number // 4), named(ordinary, number - number // 4 - 1))
    mixed = jax.random.permutation(jax.random.fold_in(own, 3), count)
    source_of, receiver = mixed[0:count // 2 * 2:2], mixed[1:count // 2 * 2:2]
    slack = jnp.minimum(sizes[source_of] - 1, bound - sizes[receiver]) // 2
    slack = jnp.where((source_of == order[0]) | (receiver == order[0]) | (sizes[receiver] == 0), 0, jnp.maximum(slack, 0))
    passed = jax.random.randint(jax.random.fold_in(own, 4), (count // 2,), 0, 1 << 20) % (slack + 1)
    sizes = sizes.at[source_of].add(-passed).at[receiver].add(passed)
    labels = jnp.searchsorted(jnp.cumsum(sizes), jnp.arange(rows * top), side="right").astype(jnp.int32)
    listing = labels.reshape(top, rows).T
    listing = listing[jax.random.permutation(jax.random.fold_in(own, 1), rows)]
    offset_by = jax.random.randint(jax.random.fold_in(own, 2), (rows, 1), 0, top)
    return jnp.take_along_axis(listing, (jnp.arange(top)[None, :] + offset_by) % top, axis=1)


def portions_of(amount, total, bound, skew, full):
    portions = [(1 << 20) // math.isqrt(rank ** skew) + 1 for rank in range(1, amount + 1)]
    largest = bound if full else min(bound, max(-(-total // amount), total * portions[0] // sum(portions)))
    least = 1 if total - largest >= amount - 1 else 0
    counts, rest = [largest] + [least] * (amount - 1), total - largest - least * (amount - 1)
    while rest > 0:
        free = [i for i in range(1, amount) if counts[i] < largest] or [i for i in range(1, amount) if counts[i] < bound]
        mass, budget = sum([portions[i] for i in free]), rest
        for i in free:
            addition = min(bound - counts[i], max(1, budget * portions[i] // mass), rest)
            counts[i] = counts[i] + addition
            rest = rest - addition
    return np.array(counts)


def centred(rng, dims, scale, most, shards=(), kind=jnp.bfloat16):
    loudness = levels(rng, dims, shards, -0.22, 0.18) if shards else 1.0
    drawn = jax.random.normal(rng, dims, jnp.float32) * scale * loudness
    return jnp.minimum(jnp.maximum(drawn, -most), most).astype(kind)


def setup_inputs(seed: int = 0) -> dict:
    key_of = jax.random.split(jax.random.key(seed), 9)
    tokens = draw_tokens(jax.random.fold_in(key_of[8], 71), 0)
    w_query = centred(key_of[1], (D, H * HD), D ** -0.5, 0.125, ((0, 64), (1, 8)))
    w_key = centred(key_of[2], (D, H * HD), D ** -0.5, 0.125, ((0, 64), (1, 8)))
    w_value = centred(key_of[3], (D, H * HD), D ** -0.5, 0.125, ((0, 64), (1, 8)))
    w_out = centred(key_of[4], (H * HD, D), (H * HD) ** -0.5, 0.125, ((0, 8), (1, 64)))
    prefix_cache = draw_prefix_cache(jax.random.fold_in(key_of[8], 71), 0)
    prefix_len = draw_prefix_len(jax.random.fold_in(key_of[8], 71), 0)
    owners_keys = jax.random.split(jax.random.fold_in(key_of[7], 1), (N_GROUP * NBLK) // NBLK)
    owners_turns = jax.random.permutation(jax.random.fold_in(key_of[7], 3), (N_GROUP * NBLK) // NBLK)
    owners = jax.vmap(lambda own, number: assign_block(jax.random.fold_in(key_of[7], 2), own, number, NBLK, N_GROUP, 1, CAP, 1))(owners_keys, owners_turns).reshape((N_GROUP * NBLK, 1))
    return dict(tokens=tokens, w_query=w_query, w_key=w_key, w_value=w_value, w_out=w_out, prefix_cache=prefix_cache, prefix_len=prefix_len, owners=owners)


def attend(query, new_key, new_value, prefix, plen):
    rows, width = query.shape
    heads = width // HD
    pre = prefix.shape[1]
    keys = jnp.concatenate([prefix[0], new_key], 0).reshape(pre + rows, heads, HD).astype(jnp.float32)
    values = jnp.concatenate([prefix[1], new_value], 0).reshape(pre + rows, heads, HD).astype(jnp.float32)
    qmat = query.reshape(rows, heads, HD).astype(jnp.float32)
    scores = jnp.einsum('chd,khd->hck', qmat, keys) * (HD ** -0.5)
    kpos = jnp.arange(pre + rows)[None, :]
    cpos = jnp.arange(rows)[:, None]
    valid = jnp.where(kpos < pre, kpos < plen, kpos - pre <= cpos)
    scores = jnp.where(valid[None], scores, -jnp.inf)
    top = jnp.max(scores, axis=-1, keepdims=True)
    expo = jnp.exp(scores - top)
    weights = (expo / jnp.sum(expo, axis=-1, keepdims=True)).astype(jnp.bfloat16)
    context = jnp.einsum('hck,khd->chd', weights.astype(jnp.float32), values)
    return context.astype(jnp.bfloat16).reshape(rows, width)


def reference(tokens, w_query, w_key, w_value, w_out, prefix_cache, prefix_len, owners):
    width = H * HD

    def one_prompt(items):
        xrows, prefix, plen = items
        query = jnp.dot(xrows, w_query, preferred_element_type=jnp.float32).astype(jnp.bfloat16)
        new_key = jnp.dot(xrows, w_key, preferred_element_type=jnp.float32).astype(jnp.bfloat16)
        new_value = jnp.dot(xrows, w_value, preferred_element_type=jnp.float32).astype(jnp.bfloat16)
        context = attend(query, new_key, new_value, prefix, plen)
        result = jnp.dot(context, w_out, preferred_element_type=jnp.float32).astype(jnp.bfloat16)
        keep = (jnp.arange(PRE) < plen)[None, :, None]
        masked = jnp.where(keep, prefix, jnp.zeros_like(prefix))
        cache = jnp.concatenate([masked, jnp.stack([new_key, new_value], 0)], 1)
        blocks = cache.reshape(2, NBLK, BT, width).transpose(1, 0, 2, 3)
        return result, blocks

    results, blocks = lax.map(one_prompt, (tokens.reshape(N_GROUP, NEW_TOK, D), prefix_cache, prefix_len))
    attn_out = results.reshape(N_GROUP * NEW_TOK, D)
    own = owners[:, 0].reshape(N_GROUP, NBLK).astype(jnp.int32)
    onehot = (own[:, :, None] == jnp.arange(N_GROUP, dtype=jnp.int32)[None, None, :]).astype(jnp.int32)
    rank = jnp.cumsum(onehot, axis=1) - onehot
    slot = jnp.sum(rank * onehot, axis=-1).astype(jnp.int32)
    cols = (jnp.arange(N_GROUP, dtype=jnp.int32)[:, None] * CAP + slot).astype(jnp.int32)
    decode_cache = jnp.zeros((N_GROUP, N_GROUP * CAP, 2, BT, width), jnp.bfloat16)
    decode_cache = decode_cache.at[own, cols].set(blocks)
    return attn_out, decode_cache
```

```python
import functools

import jax
import jax.numpy as jnp
from jax import lax
from jax.experimental import pallas as pl
from jax.experimental.pallas import tpu as pltpu
from jax.sharding import PartitionSpec as P

HD = 128
NX = 4
NC = 2
JUMP = 2
MESH = pl.DeviceIdType.MESH


def gather_kernel(nz, ny, nw, *refs):
    w_refs, tok_ref, w_out, tok_out = refs[:nw], refs[nw], refs[nw + 1], refs[nw + 2]
    zs, zr, xs, xr, ds, dr, loc, ts, tr = refs[nw + 3 :]
    g, t = lax.axis_index("group"), lax.axis_index("tensor")
    z, x = g // NX, g % NX
    y, c = t // NC, t % NC
    depth = w_refs[0].shape[0]
    half, width = tok_ref.shape[0] // 2, tok_ref.shape[1]
    up, down = nz // 2, (nz - 1) // 2

    def at_z(step):
        return ((z + step + nz) % nz * NX + x, t)

    def at_x(step):
        return (z * NX + (x + step + NX) % NX, t)

    def at_y(step):
        return (g, (y + step + ny) % ny * NC + c)

    sibling = (g, y * NC + (1 - c))

    mine = pl.ds(pl.multiple_of(g * depth, depth), depth)
    own_copies = [
        pltpu.make_async_copy(ref, w_out.at[i, mine, :], loc.at[i])
        for i, ref in enumerate(w_refs)
    ]
    own_copies.append(
        pltpu.make_async_copy(
            tok_ref, tok_out.at[:, pl.ds(pl.multiple_of(t * width, width), width)], loc.at[nw]
        )
    )
    for copy in own_copies:
        copy.start()

    peers = [at_z(j) for j in range(1, JUMP + 1)] + [at_z(-j) for j in range(1, JUMP + 1)]
    peers += [at_x(1), at_x(-1), at_y(1), at_y(-1), sibling]
    barrier = pltpu.get_barrier_semaphore()
    for peer in peers:
        pl.semaphore_signal(barrier, inc=1, device_id=peer, device_id_type=MESH)
    for copy in own_copies:
        copy.wait()
    pl.semaphore_wait(barrier, len(peers))

    started = []

    def send(src, dst, ssem, rsem, peer):
        copy = pltpu.make_async_remote_copy(
            src_ref=src, dst_ref=dst, send_sem=ssem, recv_sem=rsem,
            device_id=peer, device_id_type=MESH,
        )
        copy.start()
        started.append(copy)

    def arrived(dst, rsem):
        pltpu.make_async_copy(dst, dst, rsem).wait()

    def z_of(k):
        return (z - k + nz) % nz if k <= up else (z + (k - up)) % nz

    def rows(k, step_x):
        owner = z_of(k) * NX + (x + step_x + NX) % NX
        return w_out.at[:, pl.ds(pl.multiple_of(owner * depth, depth), depth), :]

    def along_z(k, d, sign, most):
        src = rows(k, 0)
        for j in range(min(JUMP, most - d), 0, -1):
            kk = (d + j) if sign > 0 else up + d + j
            send(src, rows(k, 0), zs.at[kk], zr.at[kk], at_z(sign * j))

    def along_x(k):
        src = rows(k, 0)
        send(src, rows(k, 0), xs.at[0, k], xr.at[0, k], at_x(1))
        send(src, rows(k, 0), xs.at[1, k], xr.at[1, k], at_x(-1))

    def across_x(k):
        arrived(rows(k, -1), xr.at[0, k])
        arrived(rows(k, 1), xr.at[1, k])
        if k % 2 == 0:
            send(rows(k, -1), rows(k, -1), ds.at[k], dr.at[k], at_x(1))
        else:
            send(rows(k, 1), rows(k, 1), ds.at[k], dr.at[k], at_x(-1))

    def tokens(step_y, h, core):
        owner = (y + step_y + ny) % ny * NC + core
        return tok_out.at[
            pl.ds(h * half, half), pl.ds(pl.multiple_of(owner * width, width), width)
        ]

    def to_sibling(step_y, h, n):
        send(tokens(step_y, h, c), tokens(step_y, h, c), ts.at[n], tr.at[n], sibling)

    along_z(0, 0, 1, up)
    along_z(0, 0, -1, down)
    along_x(0)
    for h in range(2):
        send(tokens(0, h, c), tokens(0, h, c), ts.at[h], tr.at[h], at_y(1))
        send(tokens(0, 1 - h, c), tokens(0, 1 - h, c), ts.at[3 - h], tr.at[3 - h], at_y(-1))
    for h in range(2):
        to_sibling(0, h, 6 + h)

    def token_step(n):
        if n == 0:
            arrived(tokens(-1, 0, c), tr.at[0])
            send(tokens(-1, 0, c), tokens(-1, 0, c), ts.at[4], tr.at[4], at_y(1))
            to_sibling(-1, 0, 8)
            arrived(tokens(1, 1, c), tr.at[3])
            send(tokens(1, 1, c), tokens(1, 1, c), ts.at[5], tr.at[5], at_y(-1))
            to_sibling(1, 1, 11)
        elif n == 1:
            arrived(tokens(-1, 1, c), tr.at[1])
            to_sibling(-1, 1, 9)
            arrived(tokens(1, 0, c), tr.at[2])
            to_sibling(1, 0, 10)
        else:
            for h in range(2):
                arrived(tokens(2, h, c), tr.at[4 + h])
                to_sibling(2, h, 12 + h)

    behind = [0]
    for d in range(1, up + 1):
        ahead = []
        for sign, most in ((1, up), (-1, down)):
            if d > most:
                continue
            k = d if sign > 0 else up + d
            arrived(rows(k, 0), zr.at[k])
            if d % JUMP == 0 and d < most:
                along_z(k, d, sign, most)
            along_x(k)
            ahead.append(k)
        for k in behind:
            across_x(k)
        behind = ahead
        if d in (up // 2 - 1, up // 2 + 1, up - 1):
            token_step((up // 2 - 1, up // 2 + 1, up - 1).index(d))
    for k in behind:
        across_x(k)
    for k in range(nz):
        arrived(rows(k, 2), dr.at[k])
    for n, step_y in enumerate((0, 0, -1, -1, 1, 1, 2, 2)):
        arrived(tokens(step_y, n % 2, 1 - c), tr.at[6 + n])
    for copy in started:
        copy.wait_send()


def gather(ws, tok, nz, ny):
    nw = len(ws)
    depth, cols = ws[0].shape
    vmem, hbm = pl.BlockSpec(memory_space=pltpu.VMEM), pl.BlockSpec(memory_space=pl.ANY)
    dma = pltpu.SemaphoreType.DMA
    sent = (nz - 1 + 3 * nz) * nw * ws[0].size * 2 + 7 * tok.size * 2
    return pl.pallas_call(
        functools.partial(gather_kernel, nz, ny, nw),
        out_shape=[
            jax.ShapeDtypeStruct((nw, depth * nz * NX, cols), tok.dtype),
            jax.ShapeDtypeStruct((tok.shape[0], tok.shape[1] * ny * NC), tok.dtype),
        ],
        in_specs=[hbm] * (nw + 1),
        out_specs=[vmem] * 2,
        scratch_shapes=[
            dma((nz,)), dma((nz,)), dma((2, nz)), dma((2, nz)), dma((nz,)), dma((nz,)),
            dma((nw + 1,)), dma((14,)), dma((14,)),
        ],
        compiler_params=pltpu.CompilerParams(
            collective_id=0, has_side_effects=True, vmem_limit_bytes=24 << 20
        ),
        cost_estimate=pl.CostEstimate(flops=0, bytes_accessed=2 * sent, transcendentals=0),
    )(*ws, tok)


def pack_kernel(groups, cap, own_ref, plen_ref, tok_ref, w_ref, pre_ref, fresh_ref, send_ref, count):
    pre = pre_ref.shape[1]
    block = send_ref.shape[2]
    pre_blocks = pre // block
    nblk = own_ref.shape[0]
    send_ref[...] = jnp.zeros_like(send_ref)
    for kind in range(2):
        fresh_ref[kind] = jnp.dot(
            tok_ref[...], w_ref[kind], preferred_element_type=jnp.float32
        ).astype(fresh_ref.dtype)

    @pl.loop(0, groups)
    def _(i):
        count[i] = 0

    def slot_of(b):
        owner = own_ref[b, 0]
        rank = count[owner]
        count[owner] = rank + 1
        return owner * cap + rank

    plen = plen_ref[0]

    @pl.loop(0, pre_blocks)
    def _(b):
        slot = slot_of(b)
        row = pl.multiple_of(b * block, block)
        kept = lax.broadcasted_iota(jnp.int32, (block, pre_ref.shape[2]), 0) + row < plen
        for kind in range(2):
            rows = pre_ref[kind, pl.ds(row, block), :]
            send_ref[slot, kind] = jnp.where(kept, rows, jnp.zeros_like(rows))

    @pl.loop(0, nblk - pre_blocks)
    def _(b):
        slot = slot_of(b + pre_blocks)
        row = pl.multiple_of(b * block, block)
        for kind in range(2):
            send_ref[slot, kind] = fresh_ref[kind, pl.ds(row, block), :]


def pack(owners, prefix_len, tokens, w, prefix, groups, cap):
    nblk = owners.shape[0]
    rows, width = tokens.shape[0], prefix.shape[2]
    block = (prefix.shape[1] + rows) // nblk
    vmem = pl.BlockSpec(memory_space=pltpu.VMEM)
    smem = pl.BlockSpec(memory_space=pltpu.SMEM)
    return pl.pallas_call(
        functools.partial(pack_kernel, groups, cap),
        out_shape=[
            jax.ShapeDtypeStruct((2, rows, width), tokens.dtype),
            jax.ShapeDtypeStruct((groups * cap, 2, block, width), tokens.dtype),
        ],
        in_specs=[smem, smem, vmem, vmem, vmem],
        out_specs=[vmem, vmem],
        scratch_shapes=[pltpu.SMEM((groups,), jnp.int32)],
        compiler_params=pltpu.CompilerParams(vmem_limit_bytes=32 << 20),
        cost_estimate=pl.CostEstimate(
            flops=4 * rows * tokens.shape[1] * width, bytes_accessed=8 << 20, transcendentals=0
        ),
    )(owners, prefix_len, tokens, w, prefix)


def attend(query, new_key, new_value, prefix, plen):
    rows, width = query.shape
    heads = width // HD
    pre = prefix.shape[1]
    keys = jnp.concatenate([prefix[0], new_key], 0).reshape(pre + rows, heads, HD)
    values = jnp.concatenate([prefix[1], new_value], 0).reshape(pre + rows, heads, HD)
    qmat = query.reshape(rows, heads, HD)
    scores = jnp.einsum("chd,khd->hck", qmat, keys, preferred_element_type=jnp.float32) * HD ** (
        -0.5
    )
    kpos = jnp.arange(pre + rows)[None, :]
    cpos = jnp.arange(rows)[:, None]
    valid = jnp.where(kpos < pre, kpos < plen, kpos - pre <= cpos)
    scores = jnp.where(valid[None], scores, -jnp.inf)
    top = jnp.max(scores, axis=-1, keepdims=True)
    expo = jnp.exp(scores - top)
    weights = (expo / jnp.sum(expo, axis=-1, keepdims=True)).astype(jnp.bfloat16)
    context = jnp.einsum("hck,khd->chd", weights, values, preferred_element_type=jnp.float32)
    return context.astype(jnp.bfloat16).reshape(rows, width)


def body(tokens, w_query, w_key, w_value, w_out, prefix_cache, prefix_len, owners):
    groups, tensors = lax.axis_size("group"), lax.axis_size("tensor")
    nz, ny = groups // NX, tensors // NC
    w_all, whole = gather((w_key, w_value, w_query, w_out.T), tokens, nz, ny)
    prefix = prefix_cache[0]
    cap = max(2, 2 * owners.shape[0] // groups)
    fresh, send = pack(owners, prefix_len, whole, w_all, prefix, groups, cap)
    received = lax.all_to_all(send, "group", split_axis=0, concat_axis=0, tiled=True)
    decode_cache = received[None]
    query = jnp.dot(whole, w_all[2], preferred_element_type=jnp.float32).astype(jnp.bfloat16)
    context = attend(query, fresh[0], fresh[1], prefix, prefix_len[0])
    gathered = lax.dot_general(
        context, w_all[3], (((1,), (1,)), ((), ())), preferred_element_type=jnp.float32
    )
    attn_out = lax.psum_scatter(
        gathered.astype(jnp.bfloat16), "tensor", scatter_dimension=1, tiled=True
    )
    return (attn_out, decode_cache)


def solution(mesh):
    in_specs = (
        P("group", "tensor"),
        P("group", "tensor"),
        P("group", "tensor"),
        P("group", "tensor"),
        P("tensor", "group"),
        P("group", None, None, "tensor"),
        P("group"),
        P("group", None),
    )
    out_specs = (P("group", "tensor"), P("group", None, None, None, "tensor"))
    return jax.shard_map(body, mesh=mesh, in_specs=in_specs, out_specs=out_specs, check_vma=False)
```

```python
import functools

import jax
import jax.numpy as jnp
from jax import lax
from jax.experimental import pallas as pl
from jax.experimental.pallas import tpu as pltpu
from jax.sharding import PartitionSpec as P

HD = 128
NX = 4
NC = 2
JUMP = 2
TILE = 128
MESH = pl.DeviceIdType.MESH
BF16, F32 = jnp.bfloat16, jnp.float32


def kernel(nz, ny, cap, *refs):
    w_refs, tok_ref, pre_ref, plen_ref, own_ref = refs[:4], refs[4], refs[5], refs[6], refs[7]
    attn_out, cache_out = refs[8:10]
    w, tok, pre, cache, packed, where_v, where_s, query, context = refs[10:19]
    mine, sib_send, sib_recv, y_send, y_recv = refs[19:24]
    zs, zr, qzs, qzr, xs, xr, ds, dr, qxs, qxr, ts, tr, loc, bs, br, ys, yr, ex = refs[24:]

    g, t = lax.axis_index("group"), lax.axis_index("tensor")
    z, x = g // NX, g % NX
    y, c = t // NC, t % NC
    groups = nz * NX
    rows_n, width = tok_ref.shape
    half = rows_n // 2
    pre_n = pre_ref.shape[2]
    nblk = own_ref.shape[0]
    block = (pre_n + rows_n) // nblk
    up, down = nz // 2, (nz - 1) // 2

    def at_z(step):
        return ((z + step + nz) % nz * NX + x, t)

    def at_x(step):
        return (z * NX + (x + step + NX) % NX, t)

    def at_y(step):
        return (g, (y + step + ny) % ny * NC + c)

    sibling = (g, y * NC + (1 - c))

    own_copies = [
        pltpu.make_async_copy(ref, w.at[i, z, x], loc.at[i]) for i, ref in enumerate(w_refs)
    ]
    own_copies.append(
        pltpu.make_async_copy(
            tok_ref, tok.at[:, pl.ds(pl.multiple_of(t * width, width), width)], loc.at[4]
        )
    )
    own_pre = pltpu.make_async_copy(pre_ref.at[0], pre, loc.at[5])
    for copy in own_copies + [own_pre]:
        copy.start()

    barrier = pltpu.get_barrier_semaphore()

    @pl.loop(1, groups)
    def _(i):
        pl.semaphore_signal(barrier, inc=1, device_id=((g + i) % groups, t), device_id_type=MESH)

    for peer in [at_y(i) for i in range(1, ny)] + [sibling]:
        pl.semaphore_signal(barrier, inc=1, device_id=peer, device_id_type=MESH)
    for copy in own_copies:
        copy.wait()
    pl.semaphore_wait(barrier, groups - 1 + ny)

    started = []

    def send(src, dst, ssem, rsem, peer):
        copy = pltpu.make_async_remote_copy(
            src_ref=src, dst_ref=dst, send_sem=ssem, recv_sem=rsem,
            device_id=peer, device_id_type=MESH,
        )
        copy.start()
        started.append(copy)

    def arrived(dst, rsem):
        pltpu.make_async_copy(dst, dst, rsem).wait()

    def z_of(k):
        return (z - k + nz) % nz if k <= up else (z + (k - up)) % nz

    def kv(k, step_x):
        return w.at[pl.ds(0, 2), z_of(k), (x + step_x + NX) % NX]

    def qo(k):
        return w.at[pl.ds(2, 2), z_of(k), x]

    def along_z(item, k, d, sign, most, ssem, rsem):
        for j in range(min(JUMP, most - d), 0, -1):
            kk = (d + j) if sign > 0 else up + d + j
            send(item(k), item(k), ssem.at[kk], rsem.at[kk], at_z(sign * j))

    def kv_here(k):
        return kv(k, 0)

    def along_x(k):
        send(kv(k, 0), kv(k, 0), xs.at[0, k], xr.at[0, k], at_x(1))
        send(kv(k, 0), kv(k, 0), xs.at[1, k], xr.at[1, k], at_x(-1))

    def across_x(k):
        arrived(kv(k, -1), xr.at[0, k])
        arrived(kv(k, 1), xr.at[1, k])
        if k % 2 == 0:
            send(kv(k, -1), kv(k, -1), ds.at[k], dr.at[k], at_x(1))
        else:
            send(kv(k, 1), kv(k, 1), ds.at[k], dr.at[k], at_x(-1))

    def tokens(step_y, h, core):
        owner = (y + step_y + ny) % ny * NC + core
        return tok.at[pl.ds(h * half, half), pl.ds(pl.multiple_of(owner * width, width), width)]

    def to_sibling(step_y, h, n):
        send(tokens(step_y, h, c), tokens(step_y, h, c), ts.at[n], tr.at[n], sibling)

    for sign, most in ((1, up), (-1, down)):
        along_z(kv_here, 0, 0, sign, most, zs, zr)
    along_x(0)
    for h in range(2):
        send(tokens(0, h, c), tokens(0, h, c), ts.at[h], tr.at[h], at_y(1))
        send(tokens(0, 1 - h, c), tokens(0, 1 - h, c), ts.at[3 - h], tr.at[3 - h], at_y(-1))
    for sign, most in ((1, up), (-1, down)):
        along_z(qo, 0, 0, sign, most, qzs, qzr)
    for h in range(2):
        to_sibling(0, h, 6 + h)

    owner_col = own_ref[...]
    bi = lax.broadcasted_iota(jnp.int32, (nblk, nblk), 0)
    bj = lax.broadcasted_iota(jnp.int32, (nblk, nblk), 1)
    owner_row = jnp.sum(jnp.where(bi == bj, owner_col, 0), axis=0, keepdims=True)
    rank = jnp.sum(
        jnp.where((owner_col == owner_row) & (bj < bi), 1, 0), axis=1, keepdims=True
    )
    slot = owner_col * cap + rank
    si = lax.broadcasted_iota(jnp.int32, (nblk, groups * cap), 1)
    sb = lax.broadcasted_iota(jnp.int32, (nblk, groups * cap), 0)
    where_v[...] = nblk - jnp.sum(jnp.where(slot == si, nblk - sb, 0), axis=0, keepdims=True)
    slots = pltpu.make_async_copy(where_v, where_s, loc.at[6])
    slots.start()

    own_pre.wait()
    plen = plen_ref[0]
    filled = lax.broadcasted_iota(jnp.int32, (pre_n, width), 0) < plen
    for kind in range(2):
        rows = pre[kind]
        cache[kind, pl.ds(0, pre_n // block)] = jnp.where(
            filled, rows, jnp.zeros_like(rows)
        ).reshape(pre_n // block, block, width)
        cache[kind, nblk] = jnp.zeros((block, width), cache.dtype)
    slots.wait()

    def token_step(n):
        if n == 0:
            arrived(tokens(-1, 0, c), tr.at[0])
            send(tokens(-1, 0, c), tokens(-1, 0, c), ts.at[4], tr.at[4], at_y(1))
            to_sibling(-1, 0, 8)
            arrived(tokens(1, 1, c), tr.at[3])
            send(tokens(1, 1, c), tokens(1, 1, c), ts.at[5], tr.at[5], at_y(-1))
            to_sibling(1, 1, 11)
        elif n == 1:
            arrived(tokens(-1, 1, c), tr.at[1])
            to_sibling(-1, 1, 9)
            arrived(tokens(1, 0, c), tr.at[2])
            to_sibling(1, 0, 10)
        else:
            for h in range(2):
                arrived(tokens(2, h, c), tr.at[4 + h])
                to_sibling(2, h, 12 + h)

    behind = [(0, 0, 1, 0)]
    token_at = (up // 2 - 1, up // 2 + 1, up - 1)
    for d in range(1, up + 2):
        ahead = []
        for sign, most in ((1, up), (-1, down)):
            if d > most:
                continue
            k = d if sign > 0 else up + d
            arrived(kv(k, 0), zr.at[k])
            if d % JUMP == 0 and d < most:
                along_z(kv_here, k, d, sign, most, zs, zr)
            along_x(k)
            ahead.append((k, d, sign, most))
        for k, dd, sign, most in behind:
            across_x(k)
            if k:
                arrived(qo(k), qzr.at[k])
                if dd % JUMP == 0 and dd < most:
                    along_z(qo, k, dd, sign, most, qzs, qzr)
        behind = ahead
        if d in token_at:
            token_step(token_at.index(d))

    for n, step in enumerate((1, -1, 2)):
        ref = w.at[pl.ds(2, 2), :, x]
        send(ref, ref, qxs.at[n], qxr.at[n], at_x(step))
    for k in range(nz):
        arrived(kv(k, 2), dr.at[k])
    for n, step_y in enumerate((0, 0, -1, -1, 1, 1, 2, 2)):
        arrived(tokens(step_y, n % 2, 1 - c), tr.at[6 + n])

    def project(i):
        return jnp.dot(
            tok[...], w[i].reshape(tok.shape[1], width), preferred_element_type=F32
        ).astype(BF16)

    for kind in range(2):
        cache[kind, pl.ds(pre_n // block, rows_n // block)] = project(kind).reshape(
            rows_n // block, block, width
        )

    @pl.loop(0, groups * cap)
    def _(s):
        b = where_s[0, s]
        for kind in range(2):
            packed[s, kind] = cache[kind, b]

    def exchange(step_z, step_x):
        peer = (z + step_z) % nz * NX + (x + step_x) % NX
        return pltpu.make_async_remote_copy(
            src_ref=packed.at[pl.ds(peer * cap, cap)],
            dst_ref=cache_out.at[pl.ds(g * cap, cap)],
            send_sem=ex.at[0], recv_sem=ex.at[1],
            device_id=(peer, t), device_id_type=MESH,
        )

    keep = pltpu.make_async_copy(
        packed.at[pl.ds(g * cap, cap)], cache_out.at[pl.ds(g * cap, cap)], loc.at[7]
    )
    keep.start()
    for step_x in (0, 1, 3, 2):

        @pl.loop(1, nz + (1 if step_x else 0))
        def _(i):
            m = nz - i
            far = (m + 1) // 2
            step_z = m % 2 * far + (1 - m % 2) * (nz - far)
            exchange(step_z, step_x).start()

    for n, step in enumerate((-1, 1, 2)):
        ref = w.at[pl.ds(2, 2), :, (x + step + NX) % NX]
        arrived(ref, qxr.at[n])
    query[...] = project(2)
    keys_n = pre_n + rows_n
    for head in range(width // HD):
        cols = pl.ds(head * HD, HD)

        @pl.loop(0, rows_n // TILE)
        def _(i):
            first = pl.multiple_of(i * TILE, TILE)
            scores = lax.dot_general(
                query[pl.ds(first, TILE), cols], cache[0, pl.ds(0, nblk), :, cols].reshape(keys_n, HD),
                (((1,), (1,)), ((), ())), preferred_element_type=F32,
            ) * HD ** (-0.5)
            kpos = lax.broadcasted_iota(jnp.int32, (TILE, keys_n), 1)
            cpos = lax.broadcasted_iota(jnp.int32, (TILE, keys_n), 0) + first
            valid = (kpos < plen) | ((kpos >= pre_n) & (kpos - pre_n <= cpos))
            scores = jnp.where(valid, scores, -jnp.inf)
            top = jnp.max(scores, axis=-1, keepdims=True)
            expo = jnp.exp(scores - top)
            weights = (expo / jnp.sum(expo, axis=-1, keepdims=True)).astype(BF16)
            context[pl.ds(first, TILE), cols] = jnp.dot(
                weights, cache[1, pl.ds(0, nblk), :, cols].reshape(keys_n, HD), preferred_element_type=F32
            ).astype(BF16)

    per = width // (NX * w_refs[3].shape[0])

    def partial(step_y, core):
        owner = (y + step_y) % ny * NC + core
        part = w[3, pl.ds(owner * per, per)].reshape(width, width)
        return lax.dot_general(
            context[...], part, (((1,), (1,)), ((), ())), preferred_element_type=F32
        )

    order = (2, 1, 3, 0)
    for step in order:
        sib_send[step] = partial(step, 1 - c).astype(BF16)
        send(sib_send.at[step], sib_recv.at[step], bs.at[step], br.at[step], sibling)
    for step in order:
        mine[step] = partial(step, c)
    for step in order:
        arrived(sib_recv.at[step], br.at[step])
        total = mine[step] + sib_recv[step].astype(F32)
        if step:
            y_send[step - 1] = total.astype(BF16)
            send(y_send.at[step - 1], y_recv.at[step - 1], ys.at[step - 1], yr.at[step - 1], at_y(step))
        else:
            mine[0] = total
    for n in (1, 0, 2):
        arrived(y_recv.at[n], yr.at[n])
    total = mine[0]
    for n in range(ny - 1):
        total = total + y_recv[n].astype(F32)
    attn_out[...] = total.astype(BF16)

    keep.wait()
    for copy in started:
        copy.wait_send()
    arrived(cache_out.at[pl.ds(0, (groups - 1) * cap)], ex.at[1])
    arrived(packed.at[pl.ds(0, (groups - 1) * cap)], ex.at[0])


def body(tokens, w_query, w_key, w_value, w_out, prefix_cache, prefix_len, owners):
    groups, tensors = lax.axis_size("group"), lax.axis_size("tensor")
    nz, ny = groups // NX, tensors // NC
    nblk = owners.shape[0]
    rows, width = tokens.shape
    depth = w_query.shape[0]
    pre_n = prefix_cache.shape[2]
    cap = max(2, 2 * nblk // groups)
    block = (pre_n + rows) // nblk
    vmem = pl.BlockSpec(memory_space=pltpu.VMEM)
    smem = pl.BlockSpec(memory_space=pltpu.SMEM)
    hbm = pl.BlockSpec(memory_space=pltpu.HBM)
    dma = pltpu.SemaphoreType.DMA
    attn_out, decode_cache = pl.pallas_call(
        functools.partial(kernel, nz, ny, cap),
        out_shape=[
            jax.ShapeDtypeStruct((rows, width), BF16),
            jax.ShapeDtypeStruct((groups * cap, 2, block, width), BF16),
        ],
        in_specs=[hbm] * 6 + [smem, vmem],
        out_specs=[vmem, vmem],
        scratch_shapes=[
            pltpu.VMEM((4, nz, NX, depth, width), BF16),
            pltpu.VMEM((rows, width * tensors), BF16),
            pltpu.VMEM((2, pre_n, width), BF16),
            pltpu.VMEM((2, nblk + 1, block, width), BF16),
            pltpu.VMEM((groups * cap, 2, block, width), BF16),
            pltpu.VMEM((1, groups * cap), jnp.int32),
            pltpu.SMEM((1, groups * cap), jnp.int32),
            pltpu.VMEM((rows, width), BF16),
            pltpu.VMEM((rows, width), BF16),
            pltpu.VMEM((ny, rows, width), F32),
            pltpu.VMEM((ny, rows, width), BF16),
            pltpu.VMEM((ny, rows, width), BF16),
            pltpu.VMEM((ny - 1, rows, width), BF16),
            pltpu.VMEM((ny - 1, rows, width), BF16),
            dma((nz,)), dma((nz,)), dma((nz,)), dma((nz,)),
            dma((2, nz)), dma((2, nz)), dma((nz,)), dma((nz,)),
            dma((3,)), dma((3,)), dma((14,)), dma((14,)), dma((8,)),
            dma((ny,)), dma((ny,)), dma((ny - 1,)), dma((ny - 1,)), dma((2,)),
        ],
        compiler_params=pltpu.CompilerParams(
            collective_id=0, has_side_effects=True, vmem_limit_bytes=48 << 20
        ),
    )(w_key, w_value, w_query, w_out.T, tokens, prefix_cache, prefix_len, owners)
    return attn_out, decode_cache[None]


def solution(mesh):
    in_specs = (
        P("group", "tensor"),
        P("group", "tensor"),
        P("group", "tensor"),
        P("group", "tensor"),
        P("tensor", "group"),
        P("group", None, None, "tensor"),
        P("group"),
        P("group", None),
    )
    out_specs = (P("group", "tensor"), P("group", None, None, None, "tensor"))
    return jax.shard_map(body, mesh=mesh, in_specs=in_specs, out_specs=out_specs, check_vma=False)
```

```python
import functools

import jax
import jax.numpy as jnp
from jax import lax
from jax.experimental import pallas as pl
from jax.experimental.pallas import tpu as pltpu
from jax.sharding import PartitionSpec as P

HD = 128
NX = 4
NC = 2
JUMP = 2
TILE = 128
MESH = pl.DeviceIdType.MESH
BF16, F32 = jnp.bfloat16, jnp.float32


def kernel(nz, ny, cap, *refs):
    w_refs, tok_ref, pre_ref, plen_ref, own_ref = refs[:4], refs[4], refs[5], refs[6], refs[7]
    attn_out, cache_out = refs[8:10]
    w, tok, pre, cache, packed, where_v, where_s, query, context = refs[10:19]
    mine, sib_send, sib_recv, y_send, y_recv = refs[19:24]
    relay = refs[24]
    zs, zr, qzs, qzr, xs, xr, ds, dr, qxs, qxr, ts, tr, loc, bs, br, ys, yr, ex = refs[25:43]
    rs, rr, fs = refs[43:]

    g, t = lax.axis_index("group"), lax.axis_index("tensor")
    z, x = g // NX, g % NX
    y, c = t // NC, t % NC
    groups = nz * NX
    rows_n, width = tok_ref.shape
    half = rows_n // 2
    pre_n = pre_ref.shape[2]
    nblk = own_ref.shape[1]
    block = (pre_n + rows_n) // nblk
    up, down = nz // 2, (nz - 1) // 2

    def at_z(step):
        return ((z + step + nz) % nz * NX + x, t)

    def at_x(step):
        return (z * NX + (x + step + NX) % NX, t)

    def at_y(step):
        return (g, (y + step + ny) % ny * NC + c)

    sibling = (g, y * NC + (1 - c))

    own_copies = [
        pltpu.make_async_copy(ref, w.at[i, z, x], loc.at[i]) for i, ref in enumerate(w_refs)
    ]
    own_copies.append(
        pltpu.make_async_copy(
            tok_ref, tok.at[:, pl.ds(pl.multiple_of(t * width, width), width)], loc.at[4]
        )
    )
    own_pre = pltpu.make_async_copy(pre_ref.at[0], pre, loc.at[5])
    for copy in own_copies + [own_pre]:
        copy.start()

    barrier = pltpu.get_barrier_semaphore()

    @pl.loop(1, groups)
    def _(i):
        pl.semaphore_signal(barrier, inc=1, device_id=((g + i) % groups, t), device_id_type=MESH)

    for peer in [at_y(i) for i in range(1, ny)] + [sibling]:
        pl.semaphore_signal(barrier, inc=1, device_id=peer, device_id_type=MESH)
    for copy in own_copies:
        copy.wait()
    pl.semaphore_wait(barrier, groups - 1 + ny)

    started = []

    def send(src, dst, ssem, rsem, peer):
        copy = pltpu.make_async_remote_copy(
            src_ref=src, dst_ref=dst, send_sem=ssem, recv_sem=rsem,
            device_id=peer, device_id_type=MESH,
        )
        copy.start()
        started.append(copy)

    def arrived(dst, rsem):
        pltpu.make_async_copy(dst, dst, rsem).wait()

    def z_of(k):
        return (z - k + nz) % nz if k <= up else (z + (k - up)) % nz

    def key_rows(k, step_x):
        return w.at[0, z_of(k), (x + step_x + NX) % NX]

    def other_rows(k):
        return w.at[pl.ds(1, 3), z_of(k), x]

    def along_z(item, k, d, sign, most, ssem, rsem):
        for j in range(min(JUMP, most - d), 0, -1):
            kk = (d + j) if sign > 0 else up + d + j
            send(item(k), item(k), ssem.at[kk], rsem.at[kk], at_z(sign * j))

    def key_here(k):
        return key_rows(k, 0)

    def along_x(k):
        send(key_rows(k, 0), key_rows(k, 0), xs.at[0, k], xr.at[0, k], at_x(1))
        send(key_rows(k, 0), key_rows(k, 0), xs.at[1, k], xr.at[1, k], at_x(-1))

    def across_x(k):
        arrived(key_rows(k, -1), xr.at[0, k])
        arrived(key_rows(k, 1), xr.at[1, k])
        if k % 2 == 0:
            send(key_rows(k, -1), key_rows(k, -1), ds.at[k], dr.at[k], at_x(1))
        else:
            send(key_rows(k, 1), key_rows(k, 1), ds.at[k], dr.at[k], at_x(-1))

    def tokens(step_y, h, core):
        owner = (y + step_y + ny) % ny * NC + core
        return tok.at[pl.ds(h * half, half), pl.ds(pl.multiple_of(owner * width, width), width)]

    def to_sibling(step_y, h, n):
        send(tokens(step_y, h, c), tokens(step_y, h, c), ts.at[n], tr.at[n], sibling)

    for sign, most in ((1, up), (-1, down)):
        along_z(key_here, 0, 0, sign, most, zs, zr)
    along_x(0)
    for h in range(2):
        send(tokens(0, h, c), tokens(0, h, c), ts.at[h], tr.at[h], at_y(1))
        send(tokens(0, 1 - h, c), tokens(0, 1 - h, c), ts.at[3 - h], tr.at[3 - h], at_y(-1))
    for sign, most in ((1, up), (-1, down)):
        along_z(other_rows, 0, 0, sign, most, qzs, qzr)
    for h in range(2):
        to_sibling(0, h, 6 + h)

    owner_row = own_ref[...]
    bi = lax.broadcasted_iota(jnp.int32, (nblk, nblk), 0)
    bj = lax.broadcasted_iota(jnp.int32, (nblk, nblk), 1)
    owner_col = jnp.sum(jnp.where(bi == bj, owner_row, 0), axis=1, keepdims=True)
    rank = jnp.sum(
        jnp.where((owner_col == owner_row) & (bj < bi), 1, 0), axis=1, keepdims=True
    )
    slot = owner_col * cap + rank
    si = lax.broadcasted_iota(jnp.int32, (nblk, groups * cap), 1)
    sb = lax.broadcasted_iota(jnp.int32, (nblk, groups * cap), 0)
    where_v[...] = nblk - jnp.sum(jnp.where(slot == si, nblk - sb, 0), axis=0, keepdims=True)
    slots = pltpu.make_async_copy(where_v, where_s, loc.at[6])
    slots.start()

    own_pre.wait()
    plen = plen_ref[0]
    filled = lax.broadcasted_iota(jnp.int32, (pre_n, width), 0) < plen
    for kind in range(2):
        rows = pre[kind]
        cache[kind, pl.ds(0, pre_n // block)] = jnp.where(
            filled, rows, jnp.zeros_like(rows)
        ).reshape(pre_n // block, block, width)
        cache[kind, nblk] = jnp.zeros((block, width), cache.dtype)
    slots.wait()

    def token_step(n):
        if n == 0:
            arrived(tokens(-1, 0, c), tr.at[0])
            send(tokens(-1, 0, c), tokens(-1, 0, c), ts.at[4], tr.at[4], at_y(1))
            to_sibling(-1, 0, 8)
            arrived(tokens(1, 1, c), tr.at[3])
            send(tokens(1, 1, c), tokens(1, 1, c), ts.at[5], tr.at[5], at_y(-1))
            to_sibling(1, 1, 11)
        elif n == 1:
            arrived(tokens(-1, 1, c), tr.at[1])
            to_sibling(-1, 1, 9)
            arrived(tokens(1, 0, c), tr.at[2])
            to_sibling(1, 0, 10)
        else:
            for h in range(2):
                arrived(tokens(2, h, c), tr.at[4 + h])
                to_sibling(2, h, 12 + h)

    behind = [(0, 0, 1, 0)]
    token_at = (up // 2 - 1, up // 2 + 1, up - 1)
    for d in range(1, up + 2):
        ahead = []
        for sign, most in ((1, up), (-1, down)):
            if d > most:
                continue
            k = d if sign > 0 else up + d
            arrived(key_rows(k, 0), zr.at[k])
            if d % JUMP == 0 and d < most:
                along_z(key_here, k, d, sign, most, zs, zr)
            along_x(k)
            ahead.append((k, d, sign, most))
        for k, dd, sign, most in behind:
            across_x(k)
            if k:
                arrived(other_rows(k), qzr.at[k])
                if dd % JUMP == 0 and dd < most:
                    along_z(other_rows, k, dd, sign, most, qzs, qzr)
        behind = ahead
        if d in token_at:
            token_step(token_at.index(d))

    def cross(first, count, n):
        ref = w.at[pl.ds(first, count), :, x]
        for i, step in enumerate((1, -1, 2)):
            send(ref, ref, qxs.at[n, i], qxr.at[n, i], at_x(step))

    def crossed(first, count, n):
        for i, step in enumerate((-1, 1, 2)):
            arrived(w.at[pl.ds(first, count), :, (x + step + NX) % NX], qxr.at[n, i])

    cross(1, 1, 0)
    for k in range(nz):
        arrived(key_rows(k, 2), dr.at[k])
    for n, step_y in enumerate((0, 0, -1, -1, 1, 1, 2, 2)):
        arrived(tokens(step_y, n % 2, 1 - c), tr.at[6 + n])

    def project(i):
        return jnp.dot(
            tok[...], w[i].reshape(tok.shape[1], width), preferred_element_type=F32
        ).astype(BF16)

    def pack(kind, peer):
        for r in range(cap):
            slot_n = peer * cap + r
            packed[kind, slot_n] = cache[kind, where_s[0, slot_n]]

    def slots_of(kind, peer):
        return packed.at[kind, pl.ds(peer * cap, cap)]

    def lands(kind, source):
        return cache_out.at[pl.ds(source * cap, cap), kind]

    def exchange(kind):
        for dx in range(NX):
            peer = (z + up) % nz * NX + (x + dx) % NX
            pack(kind, peer)
            n = (kind * 2 + dx % 2) * 2 + dx // 2
            send(slots_of(kind, peer), relay.at[n], rs.at[n], rr.at[n], at_z(1 - 2 * (dx % 2)))
        for step_x in (0, 1, 3, 2):

            @pl.loop(1, nz - (0 if step_x else 1))
            def _(i):
                m = nz - 1 - i
                far = (m + 1) // 2
                step_z = m % 2 * far + (1 - m % 2) * (nz - far)
                peer = (z + step_z) % nz * NX + (x + step_x) % NX
                pack(kind, peer)
                pltpu.make_async_remote_copy(
                    src_ref=slots_of(kind, peer), dst_ref=lands(kind, g),
                    send_sem=ex.at[kind, 0], recv_sem=ex.at[kind, 1],
                    device_id=(peer, t), device_id_type=MESH,
                ).start()

            if step_x == 1:
                for dx in range(NX):
                    n = (kind * 2 + dx % 2) * 2 + dx // 2
                    back = 1 - 2 * (dx % 2)
                    arrived(relay.at[n], rr.at[n])
                    source = (z - back + nz) % nz * NX + x
                    peer = (z - back + up + nz) % nz * NX + (x + dx) % NX
                    send(relay.at[n], lands(kind, source), fs.at[n], ex.at[kind, 1], (peer, t))
        pack(kind, g)
        keep = pltpu.make_async_copy(slots_of(kind, g), lands(kind, g), loc.at[7 + kind])
        keep.start()
        return keep

    def new_rows(kind):
        cache[kind, pl.ds(pre_n // block, rows_n // block)] = project(kind).reshape(
            rows_n // block, block, width
        )

    new_rows(0)
    keeps = [exchange(0)]
    cross(2, 2, 1)
    crossed(1, 1, 0)
    new_rows(1)
    keeps.append(exchange(1))

    crossed(2, 2, 1)
    query[...] = project(2)
    keys_n = pre_n + rows_n
    for head in range(width // HD):
        cols = pl.ds(head * HD, HD)

        @pl.loop(0, rows_n // TILE)
        def _(i):
            first = pl.multiple_of(i * TILE, TILE)
            scores = lax.dot_general(
                query[pl.ds(first, TILE), cols], cache[0, pl.ds(0, nblk), :, cols].reshape(keys_n, HD),
                (((1,), (1,)), ((), ())), preferred_element_type=F32,
            ) * HD ** (-0.5)
            kpos = lax.broadcasted_iota(jnp.int32, (TILE, keys_n), 1)
            cpos = lax.broadcasted_iota(jnp.int32, (TILE, keys_n), 0) + first
            valid = (kpos < plen) | ((kpos >= pre_n) & (kpos - pre_n <= cpos))
            scores = jnp.where(valid, scores, -jnp.inf)
            top = jnp.max(scores, axis=-1, keepdims=True)
            expo = jnp.exp(scores - top)
            weights = (expo / jnp.sum(expo, axis=-1, keepdims=True)).astype(BF16)
            context[pl.ds(first, TILE), cols] = jnp.dot(
                weights, cache[1, pl.ds(0, nblk), :, cols].reshape(keys_n, HD), preferred_element_type=F32
            ).astype(BF16)

    per = width // (NX * w_refs[3].shape[0])

    def partial(step_y, core):
        owner = (y + step_y) % ny * NC + core
        part = w[3, pl.ds(owner * per, per)].reshape(width, width)
        return lax.dot_general(
            context[...], part, (((1,), (1,)), ((), ())), preferred_element_type=F32
        )

    order = (2, 1, 3, 0)
    for step in order:
        sib_send[step] = partial(step, 1 - c).astype(BF16)
        send(sib_send.at[step], sib_recv.at[step], bs.at[step], br.at[step], sibling)
    for step in order:
        mine[step] = partial(step, c)
    for step in order:
        arrived(sib_recv.at[step], br.at[step])
        total = mine[step] + sib_recv[step].astype(F32)
        if step:
            y_send[step - 1] = total.astype(BF16)
            send(y_send.at[step - 1], y_recv.at[step - 1], ys.at[step - 1], yr.at[step - 1], at_y(step))
        else:
            mine[0] = total
    for n in (1, 0, 2):
        arrived(y_recv.at[n], yr.at[n])
    total = mine[0]
    for n in range(ny - 1):
        total = total + y_recv[n].astype(F32)
    attn_out[...] = total.astype(BF16)

    for keep in keeps:
        keep.wait()
    for copy in started:
        copy.wait_send()
    for kind in range(2):
        arrived(packed.at[kind, pl.ds(0, (groups - 1 - NX) * cap)], ex.at[kind, 0])
        arrived(cache_out.at[pl.ds(0, (groups - 1) * cap), kind], ex.at[kind, 1])


def body(tokens, w_query, w_key, w_value, w_out, prefix_cache, prefix_len, owners):
    groups, tensors = lax.axis_size("group"), lax.axis_size("tensor")
    nz, ny = groups // NX, tensors // NC
    nblk = owners.shape[0]
    rows, width = tokens.shape
    depth = w_query.shape[0]
    pre_n = prefix_cache.shape[2]
    cap = max(2, 2 * nblk // groups)
    block = (pre_n + rows) // nblk
    vmem = pl.BlockSpec(memory_space=pltpu.VMEM)
    smem = pl.BlockSpec(memory_space=pltpu.SMEM)
    hbm = pl.BlockSpec(memory_space=pl.ANY)
    dma = pltpu.SemaphoreType.DMA
    attn_out, decode_cache = pl.pallas_call(
        functools.partial(kernel, nz, ny, cap),
        out_shape=[
            pltpu.VMEM((rows, width), BF16),
            pltpu.VMEM((groups * cap, 2, block, width), BF16),
        ],
        in_specs=[hbm] * 6 + [smem, vmem],
        out_specs=[vmem, vmem],
        scratch_shapes=[
            pltpu.VMEM((4, nz, NX, depth, width), BF16),
            pltpu.VMEM((rows, width * tensors), BF16),
            pltpu.VMEM((2, pre_n, width), BF16),
            pltpu.VMEM((2, nblk + 1, block, width), BF16),
            pltpu.VMEM((2, groups * cap, block, width), BF16),
            pltpu.VMEM((1, groups * cap), jnp.int32),
            pltpu.SMEM((1, groups * cap), jnp.int32),
            pltpu.VMEM((rows, width), BF16),
            pltpu.VMEM((rows, width), BF16),
            pltpu.VMEM((ny, rows, width), F32),
            pltpu.VMEM((ny, rows, width), BF16),
            pltpu.VMEM((ny, rows, width), BF16),
            pltpu.VMEM((ny - 1, rows, width), BF16),
            pltpu.VMEM((ny - 1, rows, width), BF16),
            pltpu.VMEM((4 * 2, cap, block, width), BF16),
            dma((nz,)), dma((nz,)), dma((nz,)), dma((nz,)),
            dma((2, nz)), dma((2, nz)), dma((nz,)), dma((nz,)),
            dma((2, 3)), dma((2, 3)), dma((14,)), dma((14,)), dma((9,)),
            dma((ny,)), dma((ny,)), dma((ny - 1,)), dma((ny - 1,)), dma((2, 2)),
            dma((8,)), dma((8,)), dma((8,)),
        ],
        compiler_params=pltpu.CompilerParams(
            collective_id=0, has_side_effects=True, vmem_limit_bytes=56 << 20
        ),
    )(w_key, w_value, w_query, w_out.T, tokens, prefix_cache, prefix_len, owners.reshape(1, nblk))
    return attn_out, decode_cache[None]


def solution(mesh):
    in_specs = (
        P("group", "tensor"),
        P("group", "tensor"),
        P("group", "tensor"),
        P("group", "tensor"),
        P("tensor", "group"),
        P("group", None, None, "tensor"),
        P("group"),
        P("group", None),
    )
    out_specs = (P("group", "tensor"), P("group", None, None, None, "tensor"))
    return jax.shard_map(body, mesh=mesh, in_specs=in_specs, out_specs=out_specs, check_vma=False)
```

```python
import functools

import jax
import jax.numpy as jnp
from jax import lax
from jax.experimental import pallas as pl
from jax.experimental.pallas import tpu as pltpu
from jax.sharding import PartitionSpec as P

HD = 128
NX = 4
NC = 2
JUMP = 2
TILE = 128
MESH = pl.DeviceIdType.MESH
BF16, F32 = jnp.bfloat16, jnp.float32


def kernel(nz, ny, cap, *refs):
    w_refs, tok_ref, pre_ref, plen_ref, own_ref = refs[:4], refs[4], refs[5], refs[6], refs[7]
    attn_out, cache_out = refs[8:10]
    w, tok, pre, cache, packed, where_v, where_s, query, context = refs[10:19]
    mine, sib_send, sib_recv, y_send, y_recv = refs[19:24]
    relay = refs[24]
    zs, zr, qzs, qzr, xs, xr, ds, dr, qxs, qxr, ts, tr, loc, bs, br, ys, yr, es = refs[25:43]
    er, rs, rr, fs = refs[43:]

    g, t = lax.axis_index("group"), lax.axis_index("tensor")
    z, x = g // NX, g % NX
    y, c = t // NC, t % NC
    groups = nz * NX
    rows_n, width = tok_ref.shape
    half = rows_n // 2
    pre_n = pre_ref.shape[2]
    nblk = own_ref.shape[1]
    block = (pre_n + rows_n) // nblk
    up, down = nz // 2, (nz - 1) // 2

    def at_z(step):
        return ((z + step + nz) % nz * NX + x, t)

    def at_x(step):
        return (z * NX + (x + step + NX) % NX, t)

    def at_y(step):
        return (g, (y + step + ny) % ny * NC + c)

    sibling = (g, y * NC + (1 - c))

    own_copies = [
        pltpu.make_async_copy(ref, w.at[i, z, x], loc.at[i]) for i, ref in enumerate(w_refs)
    ]
    own_copies.append(
        pltpu.make_async_copy(
            tok_ref, tok.at[:, pl.ds(pl.multiple_of(t * width, width), width)], loc.at[4]
        )
    )
    own_pre = pltpu.make_async_copy(pre_ref.at[0], pre, loc.at[5])
    for copy in own_copies + [own_pre]:
        copy.start()

    barrier = pltpu.get_barrier_semaphore()

    @pl.loop(1, groups)
    def _(i):
        pl.semaphore_signal(barrier, inc=1, device_id=((g + i) % groups, t), device_id_type=MESH)

    for peer in [at_y(i) for i in range(1, ny)] + [sibling]:
        pl.semaphore_signal(barrier, inc=1, device_id=peer, device_id_type=MESH)
    for copy in own_copies:
        copy.wait()
    pl.semaphore_wait(barrier, groups - 1 + ny)

    started = []

    def send(src, dst, ssem, rsem, peer):
        copy = pltpu.make_async_remote_copy(
            src_ref=src, dst_ref=dst, send_sem=ssem, recv_sem=rsem,
            device_id=peer, device_id_type=MESH,
        )
        copy.start()
        started.append(copy)

    def arrived(dst, rsem):
        pltpu.make_async_copy(dst, dst, rsem).wait()

    def z_of(k):
        return (z - k + nz) % nz if k <= up else (z + (k - up)) % nz

    def key_rows(k, step_x):
        return w.at[0, z_of(k), (x + step_x + NX) % NX]

    def other_rows(k):
        return w.at[pl.ds(1, 3), z_of(k), x]

    def along_z(item, k, d, sign, most, ssem, rsem):
        for j in range(min(JUMP, most - d), 0, -1):
            kk = (d + j) if sign > 0 else up + d + j
            send(item(k), item(k), ssem.at[kk], rsem.at[kk], at_z(sign * j))

    def key_here(k):
        return key_rows(k, 0)

    def along_x(k):
        send(key_rows(k, 0), key_rows(k, 0), xs.at[0, k], xr.at[0, k], at_x(1))
        send(key_rows(k, 0), key_rows(k, 0), xs.at[1, k], xr.at[1, k], at_x(-1))

    def across_x(k):
        arrived(key_rows(k, -1), xr.at[0, k])
        arrived(key_rows(k, 1), xr.at[1, k])
        if k % 2 == 0:
            send(key_rows(k, -1), key_rows(k, -1), ds.at[k], dr.at[k], at_x(1))
        else:
            send(key_rows(k, 1), key_rows(k, 1), ds.at[k], dr.at[k], at_x(-1))

    def tokens(step_y, h, core):
        owner = (y + step_y + ny) % ny * NC + core
        return tok.at[pl.ds(h * half, half), pl.ds(pl.multiple_of(owner * width, width), width)]

    def to_sibling(step_y, h, n):
        send(tokens(step_y, h, c), tokens(step_y, h, c), ts.at[n], tr.at[n], sibling)

    for sign, most in ((1, up), (-1, down)):
        along_z(key_here, 0, 0, sign, most, zs, zr)
    along_x(0)
    for h in range(2):
        send(tokens(0, h, c), tokens(0, h, c), ts.at[h], tr.at[h], at_y(1))
        send(tokens(0, 1 - h, c), tokens(0, 1 - h, c), ts.at[3 - h], tr.at[3 - h], at_y(-1))
    for sign, most in ((1, up), (-1, down)):
        along_z(other_rows, 0, 0, sign, most, qzs, qzr)
    for h in range(2):
        to_sibling(0, h, 6 + h)

    owner_row = own_ref[...]
    bi = lax.broadcasted_iota(jnp.int32, (nblk, nblk), 0)
    bj = lax.broadcasted_iota(jnp.int32, (nblk, nblk), 1)
    owner_col = jnp.sum(jnp.where(bi == bj, owner_row, 0), axis=1, keepdims=True)
    rank = jnp.sum(
        jnp.where((owner_col == owner_row) & (bj < bi), 1, 0), axis=1, keepdims=True
    )
    slot = owner_col * cap + rank
    si = lax.broadcasted_iota(jnp.int32, (nblk, groups * cap), 1)
    sb = lax.broadcasted_iota(jnp.int32, (nblk, groups * cap), 0)
    where_v[...] = nblk - jnp.sum(jnp.where(slot == si, nblk - sb, 0), axis=0, keepdims=True)
    slots = pltpu.make_async_copy(where_v, where_s, loc.at[6])
    slots.start()

    own_pre.wait()
    plen = plen_ref[0]
    filled = lax.broadcasted_iota(jnp.int32, (pre_n, width), 0) < plen
    for kind in range(2):
        rows = pre[kind]
        cache[kind, pl.ds(0, pre_n // block)] = jnp.where(
            filled, rows, jnp.zeros_like(rows)
        ).reshape(pre_n // block, block, width)
        cache[kind, nblk] = jnp.zeros((block, width), cache.dtype)
    slots.wait()

    def token_step(n):
        if n == 0:
            arrived(tokens(-1, 0, c), tr.at[0])
            send(tokens(-1, 0, c), tokens(-1, 0, c), ts.at[4], tr.at[4], at_y(1))
            to_sibling(-1, 0, 8)
            arrived(tokens(1, 1, c), tr.at[3])
            send(tokens(1, 1, c), tokens(1, 1, c), ts.at[5], tr.at[5], at_y(-1))
            to_sibling(1, 1, 11)
        elif n == 1:
            arrived(tokens(-1, 1, c), tr.at[1])
            to_sibling(-1, 1, 9)
            arrived(tokens(1, 0, c), tr.at[2])
            to_sibling(1, 0, 10)
        else:
            for h in range(2):
                arrived(tokens(2, h, c), tr.at[4 + h])
                to_sibling(2, h, 12 + h)

    behind = [(0, 0, 1, 0)]
    token_at = (up // 2 - 1, up // 2 + 1, up - 1)
    for d in range(1, up + 2):
        ahead = []
        for sign, most in ((1, up), (-1, down)):
            if d > most:
                continue
            k = d if sign > 0 else up + d
            arrived(key_rows(k, 0), zr.at[k])
            if d % JUMP == 0 and d < most:
                along_z(key_here, k, d, sign, most, zs, zr)
            along_x(k)
            ahead.append((k, d, sign, most))
        for k, dd, sign, most in behind:
            across_x(k)
            if k:
                arrived(other_rows(k), qzr.at[k])
                if dd % JUMP == 0 and dd < most:
                    along_z(other_rows, k, dd, sign, most, qzs, qzr)
        behind = ahead
        if d in token_at:
            token_step(token_at.index(d))

    def column(first, count, n_z, size_z, step):
        return w.at[pl.ds(first, count), pl.ds(n_z, size_z), (x + step + NX) % NX]

    def cross(first, count, n):
        ref = column(first, count, 0, nz, 0)
        for i, step in enumerate((1, -1)):
            send(ref, ref, qxs.at[n, i], qxr.at[n, i], at_x(step))

    def pass_on(first, count, n):
        for i, step in enumerate((-1, 1)):
            arrived(column(first, count, 0, nz, step), qxr.at[n, i])
            ref = column(first, count, i * (nz // 2), nz // 2, step)
            send(ref, ref, qxs.at[n, 2 + i], qxr.at[n, 2 + i], at_x(-step))

    def crossed(first, count, n):
        for i in range(2):
            arrived(column(first, count, i * (nz // 2), nz // 2, 2), qxr.at[n, 2 + i])

    cross(1, 1, 0)
    for k in range(nz):
        arrived(key_rows(k, 2), dr.at[k])
    for n, step_y in enumerate((0, 0, -1, -1, 1, 1, 2, 2)):
        arrived(tokens(step_y, n % 2, 1 - c), tr.at[6 + n])

    def project(i):
        return jnp.dot(
            tok[...], w[i].reshape(tok.shape[1], width), preferred_element_type=F32
        ).astype(BF16)

    def pack(kind, peer):
        for r in range(cap):
            slot_n = peer * cap + r
            packed[kind, slot_n] = cache[kind, where_s[0, slot_n]]

    def slots_of(kind, peer):
        return packed.at[kind, pl.ds(peer * cap, cap)]

    def lands(kind, source):
        return cache_out.at[pl.ds(source * cap, cap), kind]

    columns_x = (0, 1, 3, 2)

    def part_size(j):
        return nz - 1 - (0 if columns_x[j] else 1)

    def exchange(kind, j):
        if j == 0:
            for dx in range(NX):
                peer = (z + up) % nz * NX + (x + dx) % NX
                pack(kind, peer)
                n = (kind * 2 + dx % 2) * 2 + dx // 2
                send(slots_of(kind, peer), relay.at[n], rs.at[n], rr.at[n], at_z(1 - 2 * (dx % 2)))

        @pl.loop(1, part_size(j) + 1)
        def _(i):
            m = nz - 1 - i
            far = (m + 1) // 2
            step_z = m % 2 * far + (1 - m % 2) * (nz - far)
            peer = (z + step_z) % nz * NX + (x + columns_x[j]) % NX
            pack(kind, peer)
            pltpu.make_async_remote_copy(
                src_ref=slots_of(kind, peer), dst_ref=lands(kind, g),
                send_sem=es.at[kind, j], recv_sem=er.at[kind],
                device_id=(peer, t), device_id_type=MESH,
            ).start()

    def sent(kind, j):
        arrived(packed.at[kind, pl.ds(0, part_size(j) * cap)], es.at[kind, j])

    def relays(kind):
        for dx in range(NX):
            n = (kind * 2 + dx % 2) * 2 + dx // 2
            back = 1 - 2 * (dx % 2)
            arrived(relay.at[n], rr.at[n])
            source = (z - back + nz) % nz * NX + x
            peer = (z - back + up + nz) % nz * NX + (x + dx) % NX
            send(relay.at[n], lands(kind, source), fs.at[n], er.at[kind], (peer, t))

    keeps = []

    def keep_own(kind):
        pack(kind, g)
        copy = pltpu.make_async_copy(slots_of(kind, g), lands(kind, g), loc.at[7 + kind])
        copy.start()
        keeps.append(copy)

    def new_rows(kind):
        cache[kind, pl.ds(pre_n // block, rows_n // block)] = project(kind).reshape(
            rows_n // block, block, width
        )

    new_rows(0)
    exchange(0, 0)
    cross(2, 2, 1)
    exchange(0, 1)
    keep_own(0)
    relays(0)
    pass_on(1, 1, 0)
    sent(0, 0)
    exchange(0, 2)
    crossed(1, 1, 0)
    new_rows(1)
    pass_on(2, 2, 1)
    sent(0, 1)
    exchange(0, 3)

    crossed(2, 2, 1)
    query[...] = project(2)
    keys_n = pre_n + rows_n
    for head in range(width // HD):
        cols = pl.ds(head * HD, HD)

        @pl.loop(0, rows_n // TILE)
        def _(i):
            first = pl.multiple_of(i * TILE, TILE)
            scores = lax.dot_general(
                query[pl.ds(first, TILE), cols], cache[0, pl.ds(0, nblk), :, cols].reshape(keys_n, HD),
                (((1,), (1,)), ((), ())), preferred_element_type=F32,
            ) * HD ** (-0.5)
            kpos = lax.broadcasted_iota(jnp.int32, (TILE, keys_n), 1)
            cpos = lax.broadcasted_iota(jnp.int32, (TILE, keys_n), 0) + first
            valid = (kpos < plen) | ((kpos >= pre_n) & (kpos - pre_n <= cpos))
            scores = jnp.where(valid, scores, -jnp.inf)
            top = jnp.max(scores, axis=-1, keepdims=True)
            expo = jnp.exp(scores - top)
            weights = (expo / jnp.sum(expo, axis=-1, keepdims=True)).astype(BF16)
            context[pl.ds(first, TILE), cols] = jnp.dot(
                weights, cache[1, pl.ds(0, nblk), :, cols].reshape(keys_n, HD), preferred_element_type=F32
            ).astype(BF16)

    per = width // (NX * w_refs[3].shape[0])

    def partial(step_y, core):
        owner = (y + step_y) % ny * NC + core
        part = w[3, pl.ds(owner * per, per)].reshape(width, width)
        return lax.dot_general(
            context[...], part, (((1,), (1,)), ((), ())), preferred_element_type=F32
        )

    sent(0, 2)
    exchange(1, 0)
    keep_own(1)
    order = (2, 1, 3, 0)
    for step in order:
        sib_send[step] = partial(step, 1 - c).astype(BF16)
        send(sib_send.at[step], sib_recv.at[step], bs.at[step], br.at[step], sibling)
    for step in order:
        mine[step] = partial(step, c)
    sent(0, 3)
    exchange(1, 1)
    relays(1)
    for step in order:
        arrived(sib_recv.at[step], br.at[step])
        total = mine[step] + sib_recv[step].astype(F32)
        if step:
            y_send[step - 1] = total.astype(BF16)
            send(y_send.at[step - 1], y_recv.at[step - 1], ys.at[step - 1], yr.at[step - 1], at_y(step))
        else:
            mine[0] = total
    sent(1, 0)
    exchange(1, 2)
    sent(1, 1)
    exchange(1, 3)
    for n in (1, 0, 2):
        arrived(y_recv.at[n], yr.at[n])
    total = mine[0]
    for n in range(ny - 1):
        total = total + y_recv[n].astype(F32)
    attn_out[...] = total.astype(BF16)

    for keep in keeps:
        keep.wait()
    for copy in started:
        copy.wait_send()
    for j in (2, 3):
        sent(1, j)
    for kind in range(2):
        arrived(cache_out.at[pl.ds(0, (groups - 1) * cap), kind], er.at[kind])


def body(tokens, w_query, w_key, w_value, w_out, prefix_cache, prefix_len, owners):
    groups, tensors = lax.axis_size("group"), lax.axis_size("tensor")
    nz, ny = groups // NX, tensors // NC
    nblk = owners.shape[0]
    rows, width = tokens.shape
    depth = w_query.shape[0]
    pre_n = prefix_cache.shape[2]
    cap = max(2, 2 * nblk // groups)
    block = (pre_n + rows) // nblk
    vmem = pl.BlockSpec(memory_space=pltpu.VMEM)
    smem = pl.BlockSpec(memory_space=pltpu.SMEM)
    hbm = pl.BlockSpec(memory_space=pl.ANY)
    dma = pltpu.SemaphoreType.DMA
    attn_out, decode_cache = pl.pallas_call(
        functools.partial(kernel, nz, ny, cap),
        out_shape=[
            pltpu.VMEM((rows, width), BF16),
            pltpu.VMEM((groups * cap, 2, block, width), BF16),
        ],
        in_specs=[hbm] * 6 + [smem, vmem],
        out_specs=[vmem, vmem],
        scratch_shapes=[
            pltpu.VMEM((4, nz, NX, depth, width), BF16),
            pltpu.VMEM((rows, width * tensors), BF16),
            pltpu.VMEM((2, pre_n, width), BF16),
            pltpu.VMEM((2, nblk + 1, block, width), BF16),
            pltpu.VMEM((2, groups * cap, block, width), BF16),
            pltpu.VMEM((1, groups * cap), jnp.int32),
            pltpu.SMEM((1, groups * cap), jnp.int32),
            pltpu.VMEM((rows, width), BF16),
            pltpu.VMEM((rows, width), BF16),
            pltpu.VMEM((ny, rows, width), F32),
            pltpu.VMEM((ny, rows, width), BF16),
            pltpu.VMEM((ny, rows, width), BF16),
            pltpu.VMEM((ny - 1, rows, width), BF16),
            pltpu.VMEM((ny - 1, rows, width), BF16),
            pltpu.VMEM((4 * 2, cap, block, width), BF16),
            dma((nz,)), dma((nz,)), dma((nz,)), dma((nz,)),
            dma((2, nz)), dma((2, nz)), dma((nz,)), dma((nz,)),
            dma((2, 4)), dma((2, 4)), dma((14,)), dma((14,)), dma((9,)),
            dma((ny,)), dma((ny,)), dma((ny - 1,)), dma((ny - 1,)), dma((2, NX)),
            dma((2,)), dma((8,)), dma((8,)), dma((8,)),
        ],
        compiler_params=pltpu.CompilerParams(
            collective_id=0, has_side_effects=True, vmem_limit_bytes=56 << 20
        ),
    )(w_key, w_value, w_query, w_out.T, tokens, prefix_cache, prefix_len, owners.reshape(1, nblk))
    return attn_out, decode_cache[None]


def solution(mesh):
    in_specs = (
        P("group", "tensor"),
        P("group", "tensor"),
        P("group", "tensor"),
        P("group", "tensor"),
        P("tensor", "group"),
        P("group", None, None, "tensor"),
        P("group"),
        P("group", None),
    )
    out_specs = (P("group", "tensor"), P("group", None, None, None, "tensor"))
    return jax.shard_map(body, mesh=mesh, in_specs=in_specs, out_specs=out_specs, check_vma=False)
```

```python
import functools

import jax
import jax.numpy as jnp
from jax import lax
from jax.experimental import pallas as pl
from jax.experimental.pallas import tpu as pltpu
from jax.sharding import PartitionSpec as P

HD = 128
NX = 4
NC = 2
JUMP = 2
TILE = 128
MESH = pl.DeviceIdType.MESH
BF16, F32 = jnp.bfloat16, jnp.float32


def kernel(nz, ny, cap, *refs):
    w_refs, tok_ref, pre_ref, plen_ref, own_ref = refs[:4], refs[4], refs[5], refs[6], refs[7]
    attn_out, cache_out = refs[8:10]
    w, tok, pre, cache, packed, where_v, where_s, query, context = refs[10:19]
    mine, sib_send, sib_recv, y_send, y_recv = refs[19:24]
    relay, aside = refs[24:26]
    zs, zr, qzs, qzr, xs, xr, ds, dr, qxs, qxr, ts, tr, loc, bs, br, ys, yr, es = refs[26:44]
    er, rs, rr, fs, ps, pr = refs[44:]

    g, t = lax.axis_index("group"), lax.axis_index("tensor")
    z, x = g // NX, g % NX
    y, c = t // NC, t % NC
    groups = nz * NX
    rows_n, width = tok_ref.shape
    half = rows_n // 2
    pre_n = pre_ref.shape[2]
    nblk = own_ref.shape[1]
    block = (pre_n + rows_n) // nblk
    up, down = nz // 2, (nz - 1) // 2

    def at_z(step):
        return ((z + step + nz) % nz * NX + x, t)

    def at_x(step):
        return (z * NX + (x + step + NX) % NX, t)

    def at_y(step):
        return (g, (y + step + ny) % ny * NC + c)

    sibling = (g, y * NC + (1 - c))

    own_copies = [
        pltpu.make_async_copy(ref, w.at[i, z, x], loc.at[i]) for i, ref in enumerate(w_refs)
    ]
    own_copies.append(
        pltpu.make_async_copy(
            tok_ref, tok.at[:, pl.ds(pl.multiple_of(t * width, width), width)], loc.at[4]
        )
    )
    own_pre = pltpu.make_async_copy(pre_ref.at[0], pre, loc.at[5])
    for copy in own_copies + [own_pre]:
        copy.start()

    barrier = pltpu.get_barrier_semaphore()

    peers = [at_z(i) for i in range(1, nz)] + [at_x(i) for i in range(1, NX)]
    peers += [at_y(i) for i in range(1, ny)] + [sibling]
    for peer in peers:
        pl.semaphore_signal(barrier, inc=1, device_id=peer, device_id_type=MESH)
    for copy in own_copies:
        copy.wait()
    pl.semaphore_wait(barrier, len(peers))

    started = []

    def send(src, dst, ssem, rsem, peer):
        copy = pltpu.make_async_remote_copy(
            src_ref=src, dst_ref=dst, send_sem=ssem, recv_sem=rsem,
            device_id=peer, device_id_type=MESH,
        )
        copy.start()
        started.append(copy)

    def arrived(dst, rsem):
        pltpu.make_async_copy(dst, dst, rsem).wait()

    def z_of(k):
        return (z - k + nz) % nz if k <= up else (z + (k - up)) % nz

    def key_rows(k, step_x):
        return w.at[0, z_of(k), (x + step_x + NX) % NX]

    def other_rows(k):
        return w.at[pl.ds(1, 3), z_of(k), x]

    def along_z(item, k, d, sign, most, ssem, rsem):
        for j in range(min(JUMP, most - d), 0, -1):
            kk = (d + j) if sign > 0 else up + d + j
            send(item(k), item(k), ssem.at[kk], rsem.at[kk], at_z(sign * j))

    def key_here(k):
        return key_rows(k, 0)

    def along_x(k):
        send(key_rows(k, 0), key_rows(k, 0), xs.at[0, k], xr.at[0, k], at_x(1))
        send(key_rows(k, 0), key_rows(k, 0), xs.at[1, k], xr.at[1, k], at_x(-1))

    def across_x(k):
        arrived(key_rows(k, -1), xr.at[0, k])
        arrived(key_rows(k, 1), xr.at[1, k])
        if k % 2 == 0:
            send(key_rows(k, -1), key_rows(k, -1), ds.at[k], dr.at[k], at_x(1))
        else:
            send(key_rows(k, 1), key_rows(k, 1), ds.at[k], dr.at[k], at_x(-1))

    def tokens(step_y, h, core):
        owner = (y + step_y + ny) % ny * NC + core
        return tok.at[pl.ds(h * half, half), pl.ds(pl.multiple_of(owner * width, width), width)]

    def to_sibling(step_y, h, n):
        send(tokens(step_y, h, c), tokens(step_y, h, c), ts.at[n], tr.at[n], sibling)

    for sign, most in ((1, up), (-1, down)):
        along_z(key_here, 0, 0, sign, most, zs, zr)
    along_x(0)
    for h in range(2):
        send(tokens(0, h, c), tokens(0, h, c), ts.at[h], tr.at[h], at_y(1))
        send(tokens(0, 1 - h, c), tokens(0, 1 - h, c), ts.at[3 - h], tr.at[3 - h], at_y(-1))
    for sign, most in ((1, up), (-1, down)):
        along_z(other_rows, 0, 0, sign, most, qzs, qzr)
    for h in range(2):
        to_sibling(0, h, 6 + h)

    owner_row = own_ref[...]
    bi = lax.broadcasted_iota(jnp.int32, (nblk, nblk), 0)
    bj = lax.broadcasted_iota(jnp.int32, (nblk, nblk), 1)
    owner_col = jnp.sum(jnp.where(bi == bj, owner_row, 0), axis=1, keepdims=True)
    rank = jnp.sum(
        jnp.where((owner_col == owner_row) & (bj < bi), 1, 0), axis=1, keepdims=True
    )
    slot = owner_col * cap + rank
    si = lax.broadcasted_iota(jnp.int32, (nblk, groups * cap), 1)
    sb = lax.broadcasted_iota(jnp.int32, (nblk, groups * cap), 0)
    where_v[...] = nblk - jnp.sum(jnp.where(slot == si, nblk - sb, 0), axis=0, keepdims=True)
    slots = pltpu.make_async_copy(where_v, where_s, loc.at[6])
    slots.start()

    own_pre.wait()
    plen = plen_ref[0]
    filled = lax.broadcasted_iota(jnp.int32, (pre_n, width), 0) < plen
    for kind in range(2):
        rows = pre[kind]
        cache[kind, pl.ds(0, pre_n // block)] = jnp.where(
            filled, rows, jnp.zeros_like(rows)
        ).reshape(pre_n // block, block, width)
        cache[kind, nblk] = jnp.zeros((block, width), cache.dtype)
    slots.wait()

    def token_step(n):
        if n == 0:
            arrived(tokens(-1, 0, c), tr.at[0])
            send(tokens(-1, 0, c), tokens(-1, 0, c), ts.at[4], tr.at[4], at_y(1))
            to_sibling(-1, 0, 8)
            arrived(tokens(1, 1, c), tr.at[3])
            send(tokens(1, 1, c), tokens(1, 1, c), ts.at[5], tr.at[5], at_y(-1))
            to_sibling(1, 1, 11)
        elif n == 1:
            arrived(tokens(-1, 1, c), tr.at[1])
            to_sibling(-1, 1, 9)
            arrived(tokens(1, 0, c), tr.at[2])
            to_sibling(1, 0, 10)
        else:
            for h in range(2):
                arrived(tokens(2, h, c), tr.at[4 + h])
                to_sibling(2, h, 12 + h)

    behind = [(0, 0, 1, 0)]
    token_at = (up // 2 - 1, up // 2 + 1, up - 1)
    for d in range(1, up + 2):
        ahead = []
        for sign, most in ((1, up), (-1, down)):
            if d > most:
                continue
            k = d if sign > 0 else up + d
            arrived(key_rows(k, 0), zr.at[k])
            if d % JUMP == 0 and d < most:
                along_z(key_here, k, d, sign, most, zs, zr)
            along_x(k)
            ahead.append((k, d, sign, most))
        for k, dd, sign, most in behind:
            across_x(k)
            if k:
                arrived(other_rows(k), qzr.at[k])
                if dd % JUMP == 0 and dd < most:
                    along_z(other_rows, k, dd, sign, most, qzs, qzr)
        behind = ahead
        if d in token_at:
            token_step(token_at.index(d))

    def column(first, count, n_z, size_z, step):
        return w.at[pl.ds(first, count), pl.ds(n_z, size_z), (x + step + NX) % NX]

    def cross(first, count, n):
        ref = column(first, count, 0, nz, 0)
        for i, step in enumerate((1, -1)):
            send(ref, ref, qxs.at[n, i], qxr.at[n, i], at_x(step))

    def pass_on(first, count, n):
        for i, step in enumerate((-1, 1)):
            arrived(column(first, count, 0, nz, step), qxr.at[n, i])
            ref = column(first, count, i * (nz // 2), nz // 2, step)
            send(ref, ref, qxs.at[n, 2 + i], qxr.at[n, 2 + i], at_x(-step))

    def crossed(first, count, n):
        for i in range(2):
            arrived(column(first, count, i * (nz // 2), nz // 2, 2), qxr.at[n, 2 + i])

    for k in range(nz):
        arrived(key_rows(k, 2), dr.at[k])
    for n, step_y in enumerate((0, 0, -1, -1, 1, 1, 2, 2)):
        arrived(tokens(step_y, n % 2, 1 - c), tr.at[6 + n])

    def project(i):
        return jnp.dot(
            tok[...], w[i].reshape(tok.shape[1], width), preferred_element_type=F32
        ).astype(BF16)

    columns_x = (0, 1, 3, 2)

    def pack(kind, dx):
        xi = (x + dx) % NX

        @pl.loop(0, nz)
        def _(zi):
            for r in range(cap):
                packed[kind, zi, xi, r] = cache[kind, where_s[0, (zi * NX + xi) * cap + r]]

    def lands(kind, source):
        return cache_out.at[pl.ds(source * cap, cap), kind]

    def part(kind, j, zi):
        return aside.at[kind, j - 1, zi] if j else packed.at[kind, zi, x]

    def to_columns(kind):
        for j in (1, 2, 3):
            pack(kind, columns_x[j])
            send(
                packed.at[kind, :, (x + columns_x[j]) % NX], aside.at[kind, j - 1],
                ps.at[kind, j - 1], pr.at[kind, j - 1], at_x(columns_x[j]),
            )
        pack(kind, 0)

    keeps = []

    def exchange(kind, j):
        source = z * NX + (x - columns_x[j] + NX) % NX
        if j:
            arrived(aside.at[kind, j - 1], pr.at[kind, j - 1])
        n = kind * NX + j
        send(part(kind, j, (z + up) % nz), relay.at[n], rs.at[n], rr.at[n], at_z(1 - 2 * (j % 2)))

        @pl.loop(2, nz)
        def _(i):
            m = nz - i
            far = (m + 1) // 2
            to_z = (z + m % 2 * far + (1 - m % 2) * (nz - far)) % nz
            pltpu.make_async_remote_copy(
                src_ref=part(kind, j, to_z), dst_ref=lands(kind, source),
                send_sem=es.at[kind, j], recv_sem=er.at[kind],
                device_id=(to_z * NX + x, t), device_id_type=MESH,
            ).start()

        copy = pltpu.make_async_copy(part(kind, j, z), lands(kind, source), loc.at[7 + n])
        copy.start()
        keeps.append(copy)

    def sent(kind, j):
        arrived(packed.at[kind, pl.ds(0, nz - 2), 0], es.at[kind, j])

    def relays(kind, j):
        n = kind * NX + j
        back = 1 - 2 * (j % 2)
        arrived(relay.at[n], rr.at[n])
        source = (z - back + nz) % nz * NX + (x - columns_x[j] + NX) % NX
        peer = (z - back + up + nz) % nz * NX + x
        send(relay.at[n], lands(kind, source), fs.at[n], er.at[kind], (peer, t))

    def new_rows(kind):
        cache[kind, pl.ds(pre_n // block, rows_n // block)] = project(kind).reshape(
            rows_n // block, block, width
        )

    new_rows(0)
    to_columns(0)
    exchange(0, 0)
    cross(1, 1, 0)
    cross(2, 2, 1)
    exchange(0, 1)
    relays(0, 0)
    sent(0, 0)
    exchange(0, 2)
    relays(0, 1)
    pass_on(1, 1, 0)
    pass_on(2, 2, 1)
    sent(0, 1)
    exchange(0, 3)
    relays(0, 2)
    crossed(1, 1, 0)
    new_rows(1)
    to_columns(1)
    relays(0, 3)

    crossed(2, 2, 1)
    query[...] = project(2)
    keys_n = pre_n + rows_n
    for head in range(width // HD):
        cols = pl.ds(head * HD, HD)

        @pl.loop(0, rows_n // TILE)
        def _(i):
            first = pl.multiple_of(i * TILE, TILE)
            scores = lax.dot_general(
                query[pl.ds(first, TILE), cols], cache[0, pl.ds(0, nblk), :, cols].reshape(keys_n, HD),
                (((1,), (1,)), ((), ())), preferred_element_type=F32,
            ) * HD ** (-0.5)
            kpos = lax.broadcasted_iota(jnp.int32, (TILE, keys_n), 1)
            cpos = lax.broadcasted_iota(jnp.int32, (TILE, keys_n), 0) + first
            valid = (kpos < plen) | ((kpos >= pre_n) & (kpos - pre_n <= cpos))
            scores = jnp.where(valid, scores, -jnp.inf)
            top = jnp.max(scores, axis=-1, keepdims=True)
            expo = jnp.exp(scores - top)
            weights = (expo / jnp.sum(expo, axis=-1, keepdims=True)).astype(BF16)
            context[pl.ds(first, TILE), cols] = jnp.dot(
                weights, cache[1, pl.ds(0, nblk), :, cols].reshape(keys_n, HD), preferred_element_type=F32
            ).astype(BF16)

    per = width // (NX * w_refs[3].shape[0])

    def partial(step_y, core):
        owner = (y + step_y) % ny * NC + core
        part = w[3, pl.ds(owner * per, per)].reshape(width, width)
        return lax.dot_general(
            context[...], part, (((1,), (1,)), ((), ())), preferred_element_type=F32
        )

    sent(0, 2)
    exchange(1, 0)
    order = (2, 1, 3, 0)
    for step in order:
        sib_send[step] = partial(step, 1 - c).astype(BF16)
        send(sib_send.at[step], sib_recv.at[step], bs.at[step], br.at[step], sibling)
    for step in order:
        mine[step] = partial(step, c)
    sent(0, 3)
    exchange(1, 1)
    relays(1, 0)
    for step in order:
        arrived(sib_recv.at[step], br.at[step])
        total = mine[step] + sib_recv[step].astype(F32)
        if step:
            y_send[step - 1] = total.astype(BF16)
            send(y_send.at[step - 1], y_recv.at[step - 1], ys.at[step - 1], yr.at[step - 1], at_y(step))
        else:
            mine[0] = total
    sent(1, 0)
    exchange(1, 2)
    relays(1, 1)
    sent(1, 1)
    exchange(1, 3)
    relays(1, 2)
    relays(1, 3)
    for n in (1, 0, 2):
        arrived(y_recv.at[n], yr.at[n])
    total = mine[0]
    for n in range(ny - 1):
        total = total + y_recv[n].astype(F32)
    attn_out[...] = total.astype(BF16)

    for keep in keeps:
        keep.wait()
    for copy in started:
        copy.wait_send()
    for j in (2, 3):
        sent(1, j)
    for kind in range(2):
        arrived(cache_out.at[pl.ds(0, (groups - NX) * cap), kind], er.at[kind])


def body(tokens, w_query, w_key, w_value, w_out, prefix_cache, prefix_len, owners):
    groups, tensors = lax.axis_size("group"), lax.axis_size("tensor")
    nz, ny = groups // NX, tensors // NC
    nblk = owners.shape[0]
    rows, width = tokens.shape
    depth = w_query.shape[0]
    pre_n = prefix_cache.shape[2]
    cap = max(2, 2 * nblk // groups)
    block = (pre_n + rows) // nblk
    vmem = pl.BlockSpec(memory_space=pltpu.VMEM)
    smem = pl.BlockSpec(memory_space=pltpu.SMEM)
    hbm = pl.BlockSpec(memory_space=pl.ANY)
    dma = pltpu.SemaphoreType.DMA
    attn_out, decode_cache = pl.pallas_call(
        functools.partial(kernel, nz, ny, cap),
        out_shape=[
            pltpu.VMEM((rows, width), BF16),
            pltpu.VMEM((groups * cap, 2, block, width), BF16),
        ],
        in_specs=[hbm] * 6 + [smem, vmem],
        out_specs=[vmem, vmem],
        scratch_shapes=[
            pltpu.VMEM((4, nz, NX, depth, width), BF16),
            pltpu.VMEM((rows, width * tensors), BF16),
            pltpu.VMEM((2, pre_n, width), BF16),
            pltpu.VMEM((2, nblk + 1, block, width), BF16),
            pltpu.VMEM((2, nz, NX, cap, block, width), BF16),
            pltpu.VMEM((1, groups * cap), jnp.int32),
            pltpu.SMEM((1, groups * cap), jnp.int32),
            pltpu.VMEM((rows, width), BF16),
            pltpu.VMEM((rows, width), BF16),
            pltpu.VMEM((ny, rows, width), F32),
            pltpu.VMEM((ny, rows, width), BF16),
            pltpu.VMEM((ny, rows, width), BF16),
            pltpu.VMEM((ny - 1, rows, width), BF16),
            pltpu.VMEM((ny - 1, rows, width), BF16),
            pltpu.VMEM((2 * NX, cap, block, width), BF16),
            pltpu.VMEM((2, NX - 1, nz, cap, block, width), BF16),
            dma((nz,)), dma((nz,)), dma((nz,)), dma((nz,)),
            dma((2, nz)), dma((2, nz)), dma((nz,)), dma((nz,)),
            dma((2, 4)), dma((2, 4)), dma((14,)), dma((14,)), dma((7 + 2 * NX,)),
            dma((ny,)), dma((ny,)), dma((ny - 1,)), dma((ny - 1,)), dma((2, NX)),
            dma((2,)), dma((8,)), dma((8,)), dma((8,)),
            dma((2, NX - 1)), dma((2, NX - 1)),
        ],
        compiler_params=pltpu.CompilerParams(
            collective_id=0, has_side_effects=True, vmem_limit_bytes=56 << 20
        ),
    )(w_key, w_value, w_query, w_out.T, tokens, prefix_cache, prefix_len, owners.reshape(1, nblk))
    return attn_out, decode_cache[None]


def solution(mesh):
    in_specs = (
        P("group", "tensor"),
        P("group", "tensor"),
        P("group", "tensor"),
        P("group", "tensor"),
        P("tensor", "group"),
        P("group", None, None, "tensor"),
        P("group"),
        P("group", None),
    )
    out_specs = (P("group", "tensor"), P("group", None, None, None, "tensor"))
    return jax.shard_map(body, mesh=mesh, in_specs=in_specs, out_specs=out_specs, check_vma=False)
```

```python
import functools

import jax
import jax.numpy as jnp
from jax import lax
from jax.experimental import pallas as pl
from jax.experimental.pallas import tpu as pltpu
from jax.sharding import PartitionSpec as P

HD = 128
NX = 4
NC = 2
JUMP = 2
TILE = 128
MESH = pl.DeviceIdType.MESH
BF16, F32 = jnp.bfloat16, jnp.float32


def kernel(nz, ny, cap, *refs):
    w_refs, tok_ref, pre_ref, plen_ref, own_ref = refs[:4], refs[4], refs[5], refs[6], refs[7]
    attn_out, cache_out = refs[8:10]
    w, tok, pre, cache, packed, where_v, where_s, query, context = refs[10:19]
    mine, sib_send, sib_recv, y_send, y_recv = refs[19:24]
    relay, aside = refs[24:26]
    zs, zr, qzs, qzr, xs, xr, ds, dr, qxs, qxr, ts, tr, loc, bs, br, ys, yr, es = refs[26:44]
    er, rs, rr, fs, ps, pr = refs[44:]

    g, t = lax.axis_index("group"), lax.axis_index("tensor")
    z, x = g // NX, g % NX
    y, c = t // NC, t % NC
    groups = nz * NX
    rows_n, width = tok_ref.shape
    half = rows_n // 2
    pre_n = pre_ref.shape[2]
    nblk = own_ref.shape[1]
    block = (pre_n + rows_n) // nblk
    up, down = nz // 2, (nz - 1) // 2

    def at_z(step):
        return ((z + step + nz) % nz * NX + x, t)

    def at_x(step):
        return (z * NX + (x + step + NX) % NX, t)

    def at_y(step):
        return (g, (y + step + ny) % ny * NC + c)

    sibling = (g, y * NC + (1 - c))

    own_copies = [
        pltpu.make_async_copy(ref, w.at[i, z, x], loc.at[i]) for i, ref in enumerate(w_refs)
    ]
    own_copies.append(
        pltpu.make_async_copy(
            tok_ref, tok.at[:, pl.ds(pl.multiple_of(t * width, width), width)], loc.at[4]
        )
    )
    own_pre = pltpu.make_async_copy(pre_ref.at[0], pre, loc.at[5])
    for copy in own_copies + [own_pre]:
        copy.start()

    barrier = pltpu.get_barrier_semaphore()

    peers = [at_z(i) for i in range(1, nz)] + [at_x(i) for i in range(1, NX)]
    peers += [at_y(i) for i in range(1, ny)] + [sibling]
    for peer in peers:
        pl.semaphore_signal(barrier, inc=1, device_id=peer, device_id_type=MESH)
    for copy in own_copies:
        copy.wait()
    pl.semaphore_wait(barrier, len(peers))

    started = []

    def send(src, dst, ssem, rsem, peer):
        copy = pltpu.make_async_remote_copy(
            src_ref=src, dst_ref=dst, send_sem=ssem, recv_sem=rsem,
            device_id=peer, device_id_type=MESH,
        )
        copy.start()
        started.append(copy)

    def arrived(dst, rsem):
        pltpu.make_async_copy(dst, dst, rsem).wait()

    def z_of(k):
        return (z - k + nz) % nz if k <= up else (z + (k - up)) % nz

    def key_rows(k, step_x):
        return w.at[0, z_of(k), (x + step_x + NX) % NX]

    def other_rows(k):
        return w.at[pl.ds(1, 3), z_of(k), x]

    def along_z(item, k, d, sign, most, ssem, rsem, jump):
        for j in range(min(jump, most - d), 0, -1):
            kk = (d + j) if sign > 0 else up + d + j
            send(item(k), item(k), ssem.at[kk], rsem.at[kk], at_z(sign * j))

    def key_here(k):
        return key_rows(k, 0)

    def along_x(k):
        send(key_rows(k, 0), key_rows(k, 0), xs.at[0, k], xr.at[0, k], at_x(1))
        send(key_rows(k, 0), key_rows(k, 0), xs.at[1, k], xr.at[1, k], at_x(-1))

    def across_x(k):
        arrived(key_rows(k, -1), xr.at[0, k])
        arrived(key_rows(k, 1), xr.at[1, k])
        if k % 2 == 0:
            send(key_rows(k, -1), key_rows(k, -1), ds.at[k], dr.at[k], at_x(1))
        else:
            send(key_rows(k, 1), key_rows(k, 1), ds.at[k], dr.at[k], at_x(-1))

    def tokens(step_y, h, core):
        owner = (y + step_y + ny) % ny * NC + core
        return tok.at[pl.ds(h * half, half), pl.ds(pl.multiple_of(owner * width, width), width)]

    def to_sibling(step_y, h, n):
        send(tokens(step_y, h, c), tokens(step_y, h, c), ts.at[n], tr.at[n], sibling)

    for sign, most in ((1, up), (-1, down)):
        along_z(key_here, 0, 0, sign, most, zs, zr, JUMP)
    along_x(0)
    for h in range(2):
        send(tokens(0, h, c), tokens(0, h, c), ts.at[h], tr.at[h], at_y(1))
        send(tokens(0, 1 - h, c), tokens(0, 1 - h, c), ts.at[3 - h], tr.at[3 - h], at_y(-1))
    for sign, most in ((1, up), (-1, down)):
        along_z(other_rows, 0, 0, sign, most, qzs, qzr, 1)
    for h in range(2):
        to_sibling(0, h, 6 + h)

    owner_row = own_ref[...]
    bi = lax.broadcasted_iota(jnp.int32, (nblk, nblk), 0)
    bj = lax.broadcasted_iota(jnp.int32, (nblk, nblk), 1)
    owner_col = jnp.sum(jnp.where(bi == bj, owner_row, 0), axis=1, keepdims=True)
    rank = jnp.sum(
        jnp.where((owner_col == owner_row) & (bj < bi), 1, 0), axis=1, keepdims=True
    )
    slot = owner_col * cap + rank
    si = lax.broadcasted_iota(jnp.int32, (nblk, groups * cap), 1)
    sb = lax.broadcasted_iota(jnp.int32, (nblk, groups * cap), 0)
    where_v[...] = nblk - jnp.sum(jnp.where(slot == si, nblk - sb, 0), axis=0, keepdims=True)
    slots = pltpu.make_async_copy(where_v, where_s, loc.at[6])
    slots.start()

    own_pre.wait()
    plen = plen_ref[0]
    filled = lax.broadcasted_iota(jnp.int32, (pre_n, width), 0) < plen
    for kind in range(2):
        rows = pre[kind]
        cache[kind, pl.ds(0, pre_n // block)] = jnp.where(
            filled, rows, jnp.zeros_like(rows)
        ).reshape(pre_n // block, block, width)
        cache[kind, nblk] = jnp.zeros((block, width), cache.dtype)
    slots.wait()

    def token_step(n):
        if n == 0:
            arrived(tokens(-1, 0, c), tr.at[0])
            send(tokens(-1, 0, c), tokens(-1, 0, c), ts.at[4], tr.at[4], at_y(1))
            to_sibling(-1, 0, 8)
            arrived(tokens(1, 1, c), tr.at[3])
            send(tokens(1, 1, c), tokens(1, 1, c), ts.at[5], tr.at[5], at_y(-1))
            to_sibling(1, 1, 11)
        elif n == 1:
            arrived(tokens(-1, 1, c), tr.at[1])
            to_sibling(-1, 1, 9)
            arrived(tokens(1, 0, c), tr.at[2])
            to_sibling(1, 0, 10)
        else:
            for h in range(2):
                arrived(tokens(2, h, c), tr.at[4 + h])
                to_sibling(2, h, 12 + h)

    def others_step(d):
        for sign, most in ((1, up), (-1, down)):
            if d <= most:
                k = d if sign > 0 else up + d
                arrived(other_rows(k), qzr.at[k])
                if d < most:
                    along_z(other_rows, k, d, sign, most, qzs, qzr, 1)

    behind = [0]
    token_at = (up // 2 - 1, up // 2 + 1, up - 1)
    for d in range(1, up + 2):
        ahead = []
        for sign, most in ((1, up), (-1, down)):
            if d > most:
                continue
            k = d if sign > 0 else up + d
            arrived(key_rows(k, 0), zr.at[k])
            if d % JUMP == 0 and d < most:
                along_z(key_here, k, d, sign, most, zs, zr, JUMP)
            along_x(k)
            ahead.append(k)
        for k in behind:
            across_x(k)
        behind = ahead
        if d in token_at:
            token_step(token_at.index(d))
            others_step(1 + token_at.index(d))

    def column(first, count, n_z, size_z, step):
        return w.at[pl.ds(first, count), pl.ds(n_z, size_z), (x + step + NX) % NX]

    def cross(first, count, n):
        ref = column(first, count, 0, nz, 0)
        for i, step in enumerate((1, -1)):
            send(ref, ref, qxs.at[n, i], qxr.at[n, i], at_x(step))

    def pass_on(first, count, n):
        for i, step in enumerate((-1, 1)):
            arrived(column(first, count, 0, nz, step), qxr.at[n, i])
            ref = column(first, count, i * (nz // 2), nz // 2, step)
            send(ref, ref, qxs.at[n, 2 + i], qxr.at[n, 2 + i], at_x(-step))

    def crossed(first, count, n):
        for i in range(2):
            arrived(column(first, count, i * (nz // 2), nz // 2, 2), qxr.at[n, 2 + i])

    others_step(up // 2)
    for k in range(nz):
        arrived(key_rows(k, 2), dr.at[k])
    others_step(up // 2 + 1)
    for n, step_y in enumerate((0, 0, -1, -1, 1, 1, 2, 2)):
        arrived(tokens(step_y, n % 2, 1 - c), tr.at[6 + n])

    def project(i):
        return jnp.dot(
            tok[...], w[i].reshape(tok.shape[1], width), preferred_element_type=F32
        ).astype(BF16)

    columns_x = (0, 1, 3, 2)

    def pack(kind, dx):
        xi = (x + dx) % NX

        @pl.loop(0, nz)
        def _(zi):
            for r in range(cap):
                packed[kind, zi, xi, r] = cache[kind, where_s[0, (zi * NX + xi) * cap + r]]

    def lands(kind, source):
        return cache_out.at[pl.ds(source * cap, cap), kind]

    def part(kind, j, zi):
        return aside.at[kind, j - 1, zi] if j else packed.at[kind, zi, x]

    def to_columns(kind):
        for j in (1, 2, 3):
            pack(kind, columns_x[j])
            send(
                packed.at[kind, :, (x + columns_x[j]) % NX], aside.at[kind, j - 1],
                ps.at[kind, j - 1], pr.at[kind, j - 1], at_x(columns_x[j]),
            )
        pack(kind, 0)

    keeps = []

    def exchange(kind, j):
        source = z * NX + (x - columns_x[j] + NX) % NX
        if j:
            arrived(aside.at[kind, j - 1], pr.at[kind, j - 1])
        n = kind * NX + j
        send(part(kind, j, (z + up) % nz), relay.at[n], rs.at[n], rr.at[n], at_z(1 - 2 * (j % 2)))

        @pl.loop(2, nz)
        def _(i):
            m = nz - i
            far = (m + 1) // 2
            to_z = (z + m % 2 * far + (1 - m % 2) * (nz - far)) % nz
            pltpu.make_async_remote_copy(
                src_ref=part(kind, j, to_z), dst_ref=lands(kind, source),
                send_sem=es.at[kind, j], recv_sem=er.at[kind],
                device_id=(to_z * NX + x, t), device_id_type=MESH,
            ).start()

        copy = pltpu.make_async_copy(part(kind, j, z), lands(kind, source), loc.at[7 + n])
        copy.start()
        keeps.append(copy)

    def sent(kind, j):
        arrived(packed.at[kind, pl.ds(0, nz - 2), 0], es.at[kind, j])

    def relays(kind, j):
        n = kind * NX + j
        back = 1 - 2 * (j % 2)
        arrived(relay.at[n], rr.at[n])
        source = (z - back + nz) % nz * NX + (x - columns_x[j] + NX) % NX
        peer = (z - back + up + nz) % nz * NX + x
        send(relay.at[n], lands(kind, source), fs.at[n], er.at[kind], (peer, t))

    def new_rows(kind):
        cache[kind, pl.ds(pre_n // block, rows_n // block)] = project(kind).reshape(
            rows_n // block, block, width
        )

    others_step(up // 2 + 2)
    new_rows(0)
    others_step(up // 2 + 3)
    to_columns(0)
    others_step(up)
    exchange(0, 0)
    cross(1, 1, 0)
    cross(2, 2, 1)
    exchange(0, 1)
    relays(0, 0)
    sent(0, 0)
    exchange(0, 2)
    relays(0, 1)
    pass_on(1, 1, 0)
    pass_on(2, 2, 1)
    sent(0, 1)
    exchange(0, 3)
    relays(0, 2)
    crossed(1, 1, 0)
    new_rows(1)
    to_columns(1)
    relays(0, 3)

    crossed(2, 2, 1)
    query[...] = project(2)
    keys_n = pre_n + rows_n
    for head in range(width // HD):
        cols = pl.ds(head * HD, HD)

        @pl.loop(0, rows_n // TILE)
        def _(i):
            first = pl.multiple_of(i * TILE, TILE)
            scores = lax.dot_general(
                query[pl.ds(first, TILE), cols], cache[0, pl.ds(0, nblk), :, cols].reshape(keys_n, HD),
                (((1,), (1,)), ((), ())), preferred_element_type=F32,
            ) * HD ** (-0.5)
            kpos = lax.broadcasted_iota(jnp.int32, (TILE, keys_n), 1)
            cpos = lax.broadcasted_iota(jnp.int32, (TILE, keys_n), 0) + first
            valid = (kpos < plen) | ((kpos >= pre_n) & (kpos - pre_n <= cpos))
            scores = jnp.where(valid, scores, -jnp.inf)
            top = jnp.max(scores, axis=-1, keepdims=True)
            expo = jnp.exp(scores - top)
            weights = (expo / jnp.sum(expo, axis=-1, keepdims=True)).astype(BF16)
            context[pl.ds(first, TILE), cols] = jnp.dot(
                weights, cache[1, pl.ds(0, nblk), :, cols].reshape(keys_n, HD), preferred_element_type=F32
            ).astype(BF16)

    per = width // (NX * w_refs[3].shape[0])

    def partial(step_y, core):
        owner = (y + step_y) % ny * NC + core
        part = w[3, pl.ds(owner * per, per)].reshape(width, width)
        return lax.dot_general(
            context[...], part, (((1,), (1,)), ((), ())), preferred_element_type=F32
        )

    sent(0, 2)
    exchange(1, 0)
    order = (2, 1, 3, 0)
    for step in order:
        sib_send[step] = partial(step, 1 - c).astype(BF16)
        send(sib_send.at[step], sib_recv.at[step], bs.at[step], br.at[step], sibling)
    for step in order:
        mine[step] = partial(step, c)
    sent(0, 3)
    exchange(1, 1)
    relays(1, 0)
    for step in order:
        arrived(sib_recv.at[step], br.at[step])
        total = mine[step] + sib_recv[step].astype(F32)
        if step:
            y_send[step - 1] = total.astype(BF16)
            send(y_send.at[step - 1], y_recv.at[step - 1], ys.at[step - 1], yr.at[step - 1], at_y(step))
        else:
            mine[0] = total
    sent(1, 0)
    exchange(1, 2)
    relays(1, 1)
    sent(1, 1)
    exchange(1, 3)
    relays(1, 2)
    relays(1, 3)
    for n in (1, 0, 2):
        arrived(y_recv.at[n], yr.at[n])
    total = mine[0]
    for n in range(ny - 1):
        total = total + y_recv[n].astype(F32)
    attn_out[...] = total.astype(BF16)

    for keep in keeps:
        keep.wait()
    for copy in started:
        copy.wait_send()
    for j in (2, 3):
        sent(1, j)
    for kind in range(2):
        arrived(cache_out.at[pl.ds(0, (groups - NX) * cap), kind], er.at[kind])


def body(tokens, w_query, w_key, w_value, w_out, prefix_cache, prefix_len, owners):
    groups, tensors = lax.axis_size("group"), lax.axis_size("tensor")
    nz, ny = groups // NX, tensors // NC
    nblk = owners.shape[0]
    rows, width = tokens.shape
    depth = w_query.shape[0]
    pre_n = prefix_cache.shape[2]
    cap = max(2, 2 * nblk // groups)
    block = (pre_n + rows) // nblk
    vmem = pl.BlockSpec(memory_space=pltpu.VMEM)
    smem = pl.BlockSpec(memory_space=pltpu.SMEM)
    hbm = pl.BlockSpec(memory_space=pl.ANY)
    dma = pltpu.SemaphoreType.DMA
    attn_out, decode_cache = pl.pallas_call(
        functools.partial(kernel, nz, ny, cap),
        out_shape=[
            pltpu.VMEM((rows, width), BF16),
            pltpu.VMEM((groups * cap, 2, block, width), BF16),
        ],
        in_specs=[hbm] * 6 + [smem, vmem],
        out_specs=[vmem, vmem],
        scratch_shapes=[
            pltpu.VMEM((4, nz, NX, depth, width), BF16),
            pltpu.VMEM((rows, width * tensors), BF16),
            pltpu.VMEM((2, pre_n, width), BF16),
            pltpu.VMEM((2, nblk + 1, block, width), BF16),
            pltpu.VMEM((2, nz, NX, cap, block, width), BF16),
            pltpu.VMEM((1, groups * cap), jnp.int32),
            pltpu.SMEM((1, groups * cap), jnp.int32),
            pltpu.VMEM((rows, width), BF16),
            pltpu.VMEM((rows, width), BF16),
            pltpu.VMEM((ny, rows, width), F32),
            pltpu.VMEM((ny, rows, width), BF16),
            pltpu.VMEM((ny, rows, width), BF16),
            pltpu.VMEM((ny - 1, rows, width), BF16),
            pltpu.VMEM((ny - 1, rows, width), BF16),
            pltpu.VMEM((2 * NX, cap, block, width), BF16),
            pltpu.VMEM((2, NX - 1, nz, cap, block, width), BF16),
            dma((nz,)), dma((nz,)), dma((nz,)), dma((nz,)),
            dma((2, nz)), dma((2, nz)), dma((nz,)), dma((nz,)),
            dma((2, 4)), dma((2, 4)), dma((14,)), dma((14,)), dma((7 + 2 * NX,)),
            dma((ny,)), dma((ny,)), dma((ny - 1,)), dma((ny - 1,)), dma((2, NX)),
            dma((2,)), dma((8,)), dma((8,)), dma((8,)),
            dma((2, NX - 1)), dma((2, NX - 1)),
        ],
        compiler_params=pltpu.CompilerParams(
            collective_id=0, has_side_effects=True, vmem_limit_bytes=56 << 20
        ),
    )(w_key, w_value, w_query, w_out.T, tokens, prefix_cache, prefix_len, owners.reshape(1, nblk))
    return attn_out, decode_cache[None]


def solution(mesh):
    in_specs = (
        P("group", "tensor"),
        P("group", "tensor"),
        P("group", "tensor"),
        P("group", "tensor"),
        P("tensor", "group"),
        P("group", None, None, "tensor"),
        P("group"),
        P("group", None),
    )
    out_specs = (P("group", "tensor"), P("group", None, None, None, "tensor"))
    return jax.shard_map(body, mesh=mesh, in_specs=in_specs, out_specs=out_specs, check_vma=False)
```
